32 devices in a mesh: outer: 4 (over x, core), inner: 8 (over z, y).
Axes of the slice: x: 2, y: 2, z: 4, core: 2. Of those that a mesh axis runs over, the one named last changes fastest.
Arguments:
- features: bfloat16 [12288, 512], P(('outer', 'inner')), may hold values from -6 to 6
- adj_tiles: bfloat16 [576, 128, 128], P(('outer', 'inner')), may hold values from 0 to 0.0625
- tile_src: int32 [96, 6], P(('outer', 'inner')), may hold values from 0 to 11, as said below
- send_rows: int32 [256, 128], P(('outer', 'inner')), may hold values from 0 to 383
- send_count: int32 [32, 8], P(('outer', 'inner')), may hold values from 1 to 128, as said below
- hub_rows: int32 [128], P(('outer', 'inner')), may hold values from 0 to 383, as said below
- w_self: float32 [512, 512], replicated, may hold values from -0.25 to 0.25
- w_neigh: float32 [512, 512], replicated, may hold values from -0.25 to 0.25
- out_bias: float32 [512], replicated, may hold values from -3 to 3
- cotangent: bfloat16 [12288, 512], P(('outer', 'inner')), may hold values from -6 to 6
Outputs:
- hidden_out: bfloat16 [12288, 512], P(('outer', 'inner'))
- grad_features: bfloat16 [12288, 512], P(('outer', 'inner'))
- grad_w_self: float32 [512, 512], replicated
- grad_w_neigh: float32 [512, 512], replicated
- grad_bias: float32 [512], replicated
The draws below stay inside these ranges and needn't reach their ends.
Inputs may be any that keep to these rules, and one draw needn't show every extreme that they name: `tile_src`: each partition's 3 * 6 tile slots name every one of its 12 source tiles at least once. `send_count`: on every partition one partner's count is exactly 128. `hub_rows`: the 4 hub rows of one partition are distinct.
All inputs are finite; a program needn't handle non-finite values.
Results may differ from the reference program's by a relative error of at most 0.0067.
Values may be sent and summed in bfloat16 or wider, within the bound.
No kernel may reach another device: no remote copies, remote signals or barrier semaphores. Data moves between devices by JAX's collectives and lax.ppermute only.
A program may use at most 128 MiB of HBM per device.

```python
import math
import jax
import jax.numpy as jnp
from jax import lax

D = 512
TILE = 128
ROWS_DEV = 384
HUB_DEV = 4
BLOCKS = 3
HUBS = 128
STILES = 12
TPB = 6
NODES = 12288
N_OUTER = 4
N_INNER = 8


def draw_tile_src(key, part):
    key = jax.random.fold_in(key, 11)
    ndevice = N_OUTER * N_INNER
    slots = BLOCKS * TPB

    def one_device(subkey):
        first, second = jax.random.split(subkey)
        extra = jax.random.randint(first, (slots - STILES,), 0, STILES, dtype=jnp.int32)
        values = jnp.concatenate([jnp.arange(STILES, dtype=jnp.int32), extra])
        return jax.random.permutation(second, values).reshape(BLOCKS, TPB)
    return jax.vmap(one_device)(jax.random.split(key, ndevice)).reshape(ndevice * BLOCKS, TPB).astype(jnp.int32)


def draw_send_rows(key, part):
    key = jax.random.fold_in(key, 23)
    return jax.random.randint(key, (N_OUTER * N_INNER * N_INNER, TILE), 0, ROWS_DEV, dtype=jnp.int32)


def draw_send_count(key, part):
    key = jax.random.fold_in(key, 37)
    ndevice = N_OUTER * N_INNER
    first, second = jax.random.split(key)
    counts = jax.random.randint(first, (ndevice, N_INNER), 1, TILE + 1, dtype=jnp.int32)
    fullest = jax.random.randint(second, (ndevice, 1), 0, N_INNER, dtype=jnp.int32)
    column = jnp.arange(N_INNER, dtype=jnp.int32)[None, :]
    return jnp.where(column == fullest, TILE, counts).astype(jnp.int32)


def draw_hub_rows(key, part):
    key = jax.random.fold_in(key, 41)
    ndevice = N_OUTER * N_INNER

    def one_device(subkey):
        return jax.random.permutation(subkey, ROWS_DEV)[:HUB_DEV].astype(jnp.int32)
    return jax.vmap(one_device)(jax.random.split(key, ndevice)).reshape(HUBS).astype(jnp.int32)


def block_scale(own_key, dims, cuts, low, top_value):
    loudness, own = 1.0, jax.random.fold_in(own_key, 6)
    for axis_at, parts in cuts:
        steps = jnp.exp(jax.random.uniform(jax.random.fold_in(own, axis_at), (parts,), jnp.float32, low / len(cuts), top_value / len(cuts)))
        loudness = loudness * jnp.repeat(steps, dims[axis_at] // parts).reshape([-1 if axis == axis_at else 1 for axis in range(len(dims))])
    return loudness


def normal_values(rng, dims, spread, limit, cuts=(), held_as=jnp.bfloat16):
    result = jax.random.normal(rng, dims, jnp.float32) * spread
    if len(cuts) > 0:
        result = block_scale(rng, dims, cuts, -0.22, 0.18) * result
    return jnp.clip(result, min=-limit, max=limit).astype(held_as)


def setup_inputs(seed: int = 0) -> dict:
    key_list = jax.random.split(jax.random.key(seed), 11)
    features = normal_values(key_list[0], (NODES, D), 1.0, 6.0, ((0, 32),))
    adj_tiles = jnp.clip(0.0625 * jax.random.uniform(key_list[1], (N_OUTER * N_INNER * BLOCKS * TPB, TILE, TILE), jnp.float32) ** block_scale(key_list[1], (N_OUTER * N_INNER * BLOCKS * TPB, TILE, TILE), ((0, 32),), -0.2, 0.2), 0.0, 0.0625).astype(jnp.bfloat16)
    tile_src = draw_tile_src(jax.random.fold_in(key_list[10], 71), 0)
    send_rows = draw_send_rows(jax.random.fold_in(key_list[10], 71), 0)
    send_count = draw_send_count(jax.random.fold_in(key_list[10], 71), 0)
    hub_rows = draw_hub_rows(jax.random.fold_in(key_list[10], 71), 0)
    w_self = normal_values(key_list[6], (D, D), D ** -0.5, 0.25, (), jnp.float32)
    w_neigh = normal_values(key_list[7], (D, D), D ** -0.5, 0.25, (), jnp.float32)
    out_bias = normal_values(key_list[8], (D,), 0.5, 3.0, (), jnp.float32)
    cotangent = normal_values(key_list[9], (NODES, D), 1.0, 6.0, ((0, 32),))
    return dict(features=features, adj_tiles=adj_tiles, tile_src=tile_src, send_rows=send_rows, send_count=send_count, hub_rows=hub_rows, w_self=w_self, w_neigh=w_neigh, out_bias=out_bias, cotangent=cotangent)


def reference(features, adj_tiles, tile_src, send_rows, send_count, hub_rows, w_self, w_neigh, out_bias, cotangent):
    ndevice = N_OUTER * N_INNER
    self_low = w_self.astype(jnp.bfloat16)
    neigh_low = w_neigh.astype(jnp.bfloat16)
    owner_base = jnp.repeat(jnp.arange(ndevice, dtype=jnp.int32) * ROWS_DEV, HUB_DEV)
    hub_global = (hub_rows + owner_base).astype(jnp.int32)
    hub_feats = features[hub_global]
    rows_three = send_rows.reshape(ndevice, N_INNER, TILE)
    slot_lane = jnp.arange(TILE, dtype=jnp.int32)
    nbound = N_INNER * TILE

    def one_part(state_all, device):
        grad_all, hub_grad, sum_self, sum_neigh, sum_bias = state_all
        outer_idx = device // N_INNER
        my_inner = device % N_INNER
        partners = (outer_idx * N_INNER + jnp.arange(N_INNER, dtype=jnp.int32)).astype(jnp.int32)
        partner_rows = rows_three[partners, my_inner]
        row_mask = slot_lane[None, :] < send_count[partners, my_inner][:, None]
        global_rows = (partners[:, None] * ROWS_DEV + partner_rows).astype(jnp.int32)
        received = jnp.where(row_mask[..., None], features[global_rows], jnp.zeros((), jnp.bfloat16)).astype(jnp.bfloat16)
        own_rows = lax.dynamic_slice_in_dim(features, (device * ROWS_DEV).astype(jnp.int32), ROWS_DEV, 0)
        source = jnp.concatenate([own_rows, received.reshape(nbound, D), hub_feats], 0).reshape(STILES, TILE, D)
        tile_ids = lax.dynamic_slice_in_dim(tile_src, (device * BLOCKS).astype(jnp.int32), BLOCKS, 0)
        weights = lax.dynamic_slice_in_dim(adj_tiles, (device * BLOCKS * TPB).astype(jnp.int32), BLOCKS * TPB, 0)
        weights = weights.reshape(BLOCKS, TPB, TILE, TILE).astype(jnp.float32)
        aggregate = jnp.einsum('btij,btjd->bid', weights, source[tile_ids].astype(jnp.float32))
        aggregate = aggregate.reshape(ROWS_DEV, D).astype(jnp.bfloat16)
        pre_act = jnp.dot(own_rows, self_low, preferred_element_type=jnp.float32) + jnp.dot(aggregate, neigh_low, preferred_element_type=jnp.float32) + out_bias
        sigmoid_pre = jax.nn.sigmoid(pre_act)
        hidden_out = (pre_act * sigmoid_pre).astype(jnp.bfloat16)
        local_cot = lax.dynamic_slice_in_dim(cotangent, (device * ROWS_DEV).astype(jnp.int32), ROWS_DEV, 0)
        grad_pre = (local_cot.astype(jnp.float32) * sigmoid_pre * (1.0 + pre_act * (1.0 - sigmoid_pre))).astype(jnp.bfloat16)
        sum_self = sum_self + jnp.dot(own_rows.T, grad_pre, preferred_element_type=jnp.float32)
        sum_neigh = sum_neigh + jnp.dot(aggregate.T, grad_pre, preferred_element_type=jnp.float32)
        sum_bias = sum_bias + lax.optimization_barrier(jnp.sum(grad_pre.astype(jnp.float32), 0))
        grad_local = jnp.dot(grad_pre, self_low.T, preferred_element_type=jnp.float32)
        grad_agg = jnp.dot(grad_pre, neigh_low.T, preferred_element_type=jnp.float32).astype(jnp.bfloat16)
        contrib = jnp.einsum('btij,bid->btjd', weights, grad_agg.reshape(BLOCKS, TILE, D).astype(jnp.float32))
        grad_src = jnp.zeros((STILES, TILE, D), jnp.float32).at[tile_ids.reshape(-1)].add(contrib.reshape(BLOCKS * TPB, TILE, D))
        grad_src = grad_src.reshape(STILES * TILE, D)
        start = (device * ROWS_DEV).astype(jnp.int32)
        current = lax.dynamic_slice_in_dim(grad_all, start, ROWS_DEV, 0)
        grad_all = lax.dynamic_update_slice_in_dim(grad_all, current + grad_local + grad_src[:ROWS_DEV], start, 0)
        bound_grad = grad_src[ROWS_DEV:ROWS_DEV + nbound].reshape(N_INNER, TILE, D)
        bound_grad = jnp.where(row_mask[..., None], bound_grad, jnp.zeros((), jnp.float32))
        grad_all = grad_all.at[global_rows.reshape(-1)].add(bound_grad.reshape(nbound, D))
        hub_grad = hub_grad + grad_src[ROWS_DEV + nbound:]
        return ((grad_all, hub_grad, sum_self, sum_neigh, sum_bias), hidden_out)
    start_state = (jnp.zeros((NODES, D), jnp.float32), jnp.zeros((HUBS, D), jnp.float32), jnp.zeros((D, D), jnp.float32), jnp.zeros((D, D), jnp.float32), jnp.zeros((D,), jnp.float32))
    final_state, hidden_all = lax.scan(one_part, start_state, jnp.arange(ndevice, dtype=jnp.int32))
    grad_all, hub_grad, sum_self, sum_neigh, sum_bias = final_state
    grad_all = grad_all.at[hub_global].add(hub_grad)
    factor = 1.0 / math.sqrt(NODES)
    return (hidden_all.reshape(NODES, D), grad_all.astype(jnp.bfloat16), sum_self * factor, sum_neigh * factor, sum_bias * factor)
```

```python
import functools

import jax
import jax.numpy as jnp
from jax import lax
from jax.experimental import pallas as pl
from jax.experimental.pallas import tpu as pltpu
from jax.sharding import PartitionSpec as P

BF = jnp.bfloat16
F32 = jnp.float32
ANY = pl.BlockSpec(memory_space=pl.ANY)
VM = pl.BlockSpec(memory_space=pltpu.VMEM)
SM = pl.BlockSpec(memory_space=pltpu.SMEM)
PARAMS = pltpu.CompilerParams(vmem_limit_bytes=48 * 1024 * 1024)
TN = (((0,), (0,)), ((), ()))
NT = (((1,), (1,)), ((), ()))


def dot(a, b, dims=(((1,), (0,)), ((), ()))):
    return lax.dot_general(a, b, dims, preferred_element_type=F32)


def tree_steps(n_outer, n_inner):
    steps = []
    for name, size in (("outer", n_outer), ("inner", n_inner)):
        bit = 1
        while bit < size:
            steps.append((name, bit))
            bit *= 2
    return steps


def tree_offsets(steps):
    count = len(steps)
    table = []
    for slot in range(2**count):
        flip = {"outer": 0, "inner": 0}
        for k, (name, bit) in enumerate(steps):
            if (slot >> (count - 1 - k)) & 1:
                flip[name] ^= bit
        table.append((flip["outer"], flip["inner"]))
    return table


def hub_order(steps, n_inner, hd, nhubs):
    me = lax.axis_index("outer") * n_inner + lax.axis_index("inner")
    column = lax.broadcasted_iota(jnp.int32, (1, nhubs), 1)
    slot = column // hd
    flip = jnp.zeros((1, nhubs), jnp.int32)
    for k, (name, bit) in enumerate(steps):
        weight = bit * n_inner if name == "outer" else bit
        flip = flip + ((slot >> (len(steps) - 1 - k)) & 1) * weight
    target = (flip ^ me) * hd + column % hd
    row = lax.broadcasted_iota(jnp.int32, (nhubs, nhubs), 0)
    return (row == target).astype(F32).astype(BF)


def load_rows(ref, at, n):
    if n % 8 == 0:
        return ref[pl.ds(pl.multiple_of(at, n), n), :]
    return jnp.concatenate([ref[pl.ds(at + r, 1), :] for r in range(n)], axis=0)


def store_rows(ref, at, value):
    n = value.shape[0]
    if n % 8 == 0:
        ref[pl.ds(pl.multiple_of(at, n), n), :] = value
    else:
        for r in range(n):
            ref[pl.ds(at + r, 1), :] = value[r : r + 1, :]


def exchange(x, name, bit):
    size = lax.axis_size(name)
    return lax.ppermute(x, name, [(s, s ^ bit) for s in range(size)])


def slot_onehot(rows_ref, count_ref, nrows):
    partners, slots = rows_ref.shape
    sub = lax.broadcasted_iota(jnp.int32, (nrows, slots), 0)
    lane = lax.broadcasted_iota(jnp.int32, (1, slots), 1)
    parts = []
    for q in range(partners):
        live = jnp.where(lane < count_ref[0, q], rows_ref[q : q + 1, :], -1)
        parts.append((sub == live).astype(F32).astype(BF))
    return jnp.concatenate(parts, axis=1)


def gather_kernel(hub_ref, count_ref, feat_ref, rows_ref, out_ref, hub_out_ref):
    nrows, width = feat_ref.shape
    partners, slots = rows_ref.shape
    nhub = hub_ref.shape[0]
    feat = feat_ref[...]
    pick = slot_onehot(rows_ref, count_ref, nrows)
    out_ref[...] = dot(pick, feat, TN).astype(BF).reshape(partners, slots, width)
    sub = lax.broadcasted_iota(jnp.int32, (16, nrows), 0)
    lane = lax.broadcasted_iota(jnp.int32, (16, nrows), 1)
    hot = jnp.zeros((16, nrows), F32)
    for h in range(nhub):
        hot = hot + ((sub == h) & (lane == hub_ref[h])).astype(F32)
    hub_out_ref[...] = dot(hot.astype(BF), feat)[:nhub]


def middle_kernel(
    steps,
    chunk,
    tile_src,
    feat_hbm,
    recv_hbm,
    hubx_hbm,
    adj_hbm,
    pre_hbm,
    wn_hbm,
    ws_hbm,
    cot_hbm,
    hidden_hbm,
    back_hbm,
    own_hbm,
    tree_hbm,
    src,
    hubx,
    hubf,
    adj,
    pre0,
    wn,
    ws,
    cot,
    agg,
    hidden,
    gsrc,
    back,
    own,
    wacc,
    tail,
    tree,
    sems,
    osems,
):
    o = lax.axis_index("outer")
    i = lax.axis_index("inner")
    n_inner = back.shape[0]
    offsets = tree_offsets(steps)
    nblocks, per_block = tile_src.shape
    tile = adj.shape[1]
    width = cot.shape[1]
    ntiles = src.shape[0]
    first_hub = nblocks + n_inner
    hd = hubx.shape[0] // len(offsets)
    pairs = [
        (hubx_hbm, hubx),
        (feat_hbm, src.at[pl.ds(0, nblocks)]),
        (recv_hbm, src.at[pl.ds(nblocks, n_inner)]),
        (adj_hbm, adj),
        (wn_hbm, wn),
        (pre_hbm, pre0),
        (cot_hbm, cot),
        (ws_hbm, ws),
    ]
    copies = [pltpu.make_async_copy(a, b, sems.at[k]) for k, (a, b) in enumerate(pairs)]
    for c in copies:
        c.start()
    outs = [
        pltpu.make_async_copy(hidden, hidden_hbm, osems.at[0]),
        pltpu.make_async_copy(back, back_hbm, osems.at[1]),
        pltpu.make_async_copy(own, own_hbm, osems.at[2]),
        pltpu.make_async_copy(tree, tree_hbm, osems.at[3]),
    ]
    devices = [(o ^ fo) * n_inner + (i ^ fi) for fo, fi in offsets]
    gsrc[...] = jnp.zeros(gsrc.shape, F32)
    copies[0].wait()
    order = hub_order(steps, n_inner, hd, hubx.shape[0])
    hubs = dot(order, hubx[...].astype(BF)).astype(BF)
    src[first_hub:] = hubs.reshape(ntiles - first_hub, tile, width)
    copies[1].wait()
    copies[2].wait()
    copies[3].wait()
    for b in range(nblocks):
        acc = jnp.zeros((tile, width), F32)
        for t in range(per_block):
            acc = acc + dot(adj[b * per_block + t], src[tile_src[b, t]])
        agg[b * tile : (b + 1) * tile, :] = acc.astype(BF)
    copies[4].wait()
    copies[5].wait()
    pre = pre0[...] + dot(agg[...], wn[...])
    copies[6].wait()
    sig = jax.nn.sigmoid(pre)
    hidden[...] = (pre * sig).astype(BF)
    outs[0].start()
    gp = (cot[...].astype(F32) * sig * (1.0 + pre * (1.0 - sig))).astype(BF)
    gagg = dot(gp, wn[...], NT).astype(BF)
    for b in range(nblocks):
        block = gagg[b * tile : (b + 1) * tile, :]
        for t in range(per_block):
            s = tile_src[b, t]
            gsrc[s] = gsrc[s] + dot(adj[b * per_block + t], block, TN)
    back[...] = gsrc[nblocks:first_hub].astype(BF)
    outs[1].start()
    feat = src[0:nblocks].reshape(nblocks * tile, width)
    wacc[0:width, :] = dot(feat, gp, TN)
    wacc[width : 2 * width, :] = dot(agg[...], gp, TN)
    hubf[...] = dot(order, gsrc[first_hub:].reshape(hubf.shape).astype(BF), TN)
    tail[...] = jnp.zeros(tail.shape, F32)
    tail[hd : hd + 1, :] = jnp.sum(gp.astype(F32), axis=0, keepdims=True)
    wrows = 2 * width // len(offsets)
    base = chunk - tail.shape[0]
    for j, d in enumerate(devices):
        mine = load_rows(wacc, d * wrows, wrows)
        if base == wrows:
            tree[j * chunk : j * chunk + wrows, :] = mine.astype(BF)
        else:
            tail[8 : 8 + wrows, :] = mine
        tail[0:hd, :] = hubf[j * hd : (j + 1) * hd, :]
        tree[j * chunk + base : (j + 1) * chunk, :] = tail[...].astype(BF)
    outs[3].start()
    copies[7].wait()
    own[...] = dot(gp, ws[...], NT) + gsrc[0:nblocks].reshape(own.shape)
    outs[2].start()
    for c in outs:
        c.wait()


def scatter_kernel(hub_ref, count_ref, rows_ref, ret_ref, own_ref, hub_grad_ref, out_ref, acc):
    nrows, width = own_ref.shape
    put = slot_onehot(rows_ref, count_ref, nrows)
    partners, slots = rows_ref.shape
    acc[...] = own_ref[...] + dot(put, ret_ref[...].reshape(partners * slots, width))
    for h in range(hub_ref.shape[0]):
        r = hub_ref[h]
        acc[pl.ds(r, 1), :] = acc[pl.ds(r, 1), :] + hub_grad_ref[h : h + 1, :]
    out_ref[...] = acc[...].astype(BF)


def finish_kernel(offsets, n_inner, factor, x_ref, self_ref, neigh_ref, full):
    o = lax.axis_index("outer")
    i = lax.axis_index("inner")
    wrows = x_ref.shape[0] // len(offsets)
    width = self_ref.shape[0]
    x = x_ref[...].astype(F32) * factor
    for j, (fo, fi) in enumerate(offsets):
        d = (o ^ fo) * n_inner + (i ^ fi)
        store_rows(full, d * wrows, x[j * wrows : (j + 1) * wrows, :])
    self_ref[...] = full[0:width, :]
    neigh_ref[...] = full[width : 2 * width, :]


def cost(flops, nbytes):
    return pl.CostEstimate(flops=flops, bytes_accessed=nbytes, transcendentals=0)


def body(
    features,
    adj_tiles,
    tile_src,
    send_rows,
    send_count,
    hub_rows,
    w_self,
    w_neigh,
    out_bias,
    cotangent,
):
    n_outer, n_inner = lax.axis_size("outer"), lax.axis_size("inner")
    ndevice = n_outer * n_inner
    nrows, width = features.shape
    tile = adj_tiles.shape[1]
    nblocks, per_block = tile_src.shape
    hd = hub_rows.shape[0]
    nhubs = hd * ndevice
    ntiles = nblocks + n_inner + nhubs // tile
    steps = tree_steps(n_outer, n_inner)
    offsets = tree_offsets(steps)
    wrows = 2 * width // ndevice
    chunk = wrows + 16 if wrows % 16 == 0 else 16
    base = chunk - 16

    outgoing, hub_own = pl.pallas_call(
        gather_kernel,
        out_shape=(
            jax.ShapeDtypeStruct((n_inner, tile, width), BF),
            jax.ShapeDtypeStruct((hd, width), F32),
        ),
        in_specs=[SM, SM, VM, VM],
        out_specs=(VM, VM),
        compiler_params=PARAMS,
        cost_estimate=cost(4 * 10**8, 3 * 10**6),
        name="gather_rows",
    )(hub_rows, send_count, features, send_rows)
    received = lax.all_to_all(outgoing, "inner", split_axis=0, concat_axis=0, tiled=True)
    hubx = hub_own
    for name, bit in reversed(steps):
        hubx = jnp.concatenate([hubx, exchange(hubx, name, bit)], 0)
    self_low = w_self.astype(BF)
    neigh_low = w_neigh.astype(BF)
    pre0 = jnp.dot(features, self_low, preferred_element_type=F32) + out_bias

    hidden_out, back, own, tree = pl.pallas_call(
        functools.partial(middle_kernel, steps, chunk),
        out_shape=(
            jax.ShapeDtypeStruct((nrows, width), BF),
            jax.ShapeDtypeStruct((n_inner, tile, width), BF),
            jax.ShapeDtypeStruct((nrows, width), F32),
            jax.ShapeDtypeStruct((ndevice * chunk, width), BF),
        ),
        in_specs=[SM] + [ANY] * 8,
        out_specs=(ANY,) * 4,
        scratch_shapes=[
            pltpu.VMEM((ntiles, tile, width), BF),
            pltpu.VMEM((nhubs, width), F32),
            pltpu.VMEM((nhubs, width), F32),
            pltpu.VMEM(adj_tiles.shape, BF),
            pltpu.VMEM((nrows, width), F32),
            pltpu.VMEM((width, width), BF),
            pltpu.VMEM((width, width), BF),
            pltpu.VMEM((nrows, width), BF),
            pltpu.VMEM((nrows, width), BF),
            pltpu.VMEM((nrows, width), BF),
            pltpu.VMEM((ntiles, tile, width), F32),
            pltpu.VMEM((n_inner, tile, width), BF),
            pltpu.VMEM((nrows, width), F32),
            pltpu.VMEM((2 * width, width), F32),
            pltpu.VMEM((16, width), F32),
            pltpu.VMEM((ndevice * chunk, width), BF),
            pltpu.SemaphoreType.DMA((8,)),
            pltpu.SemaphoreType.DMA((4,)),
        ],
        compiler_params=PARAMS,
        cost_estimate=cost(2 * 10**9, 9 * 10**6),
        name="middle",
    )(
        tile_src,
        features.reshape(nblocks, tile, width),
        received,
        hubx,
        adj_tiles,
        pre0,
        neigh_low,
        self_low,
        cotangent,
    )
    returned = lax.all_to_all(back, "inner", split_axis=0, concat_axis=0, tiled=True)
    part = tree
    for k, (name, bit) in enumerate(steps):
        half = part.shape[0] // 2
        got = exchange(part[half:], name, bit)
        part = part[:half].astype(F32) + got.astype(F32)
        if k + 1 < len(steps):
            part = part.astype(BF)
    if wrows % 16 == 0:
        mine = part[:wrows]
    else:
        mine = part[8 : 8 + wrows]
    hub_grad = part[base : base + hd]
    total_bias = part[base + hd]
    gathered = mine.astype(BF)
    for name, bit in reversed(steps):
        gathered = jnp.concatenate([gathered, exchange(gathered, name, bit)], 0)

    grad_features = pl.pallas_call(
        scatter_kernel,
        out_shape=jax.ShapeDtypeStruct((nrows, width), BF),
        in_specs=[SM, SM, VM, VM, VM, VM],
        out_specs=VM,
        scratch_shapes=[pltpu.VMEM((nrows, width), F32)],
        compiler_params=PARAMS,
        cost_estimate=cost(4 * 10**8, 3 * 10**6),
        name="scatter_rows",
    )(hub_rows, send_count, send_rows, returned, own, hub_grad)
    factor = 1.0 / float(nrows * ndevice) ** 0.5
    total_self, total_neigh = pl.pallas_call(
        functools.partial(finish_kernel, offsets, n_inner, factor),
        out_shape=(jax.ShapeDtypeStruct((width, width), F32),) * 2,
        in_specs=[VM],
        out_specs=(VM, VM),
        scratch_shapes=[pltpu.VMEM((2 * width, width), F32)],
        compiler_params=PARAMS,
        cost_estimate=cost(10**6, 3 * 10**6),
        name="finish",
    )(gathered)
    return hidden_out, grad_features, total_self, total_neigh, total_bias * factor


def solution(mesh):
    both = ("outer", "inner")
    return jax.shard_map(
        body,
        mesh=mesh,
        in_specs=(
            P(both, None),
            P(both, None, None),
            P(both, None),
            P(both, None),
            P(both, None),
            P(both),
            P(),
            P(),
            P(),
            P(both, None),
        ),
        out_specs=(P(both, None), P(both, None), P(), P(), P()),
        check_vma=False,
    )
```

```python
import functools
import math

import jax
import jax.numpy as jnp
from jax import lax
from jax.experimental import pallas as pl
from jax.experimental.pallas import tpu as pltpu
from jax.sharding import PartitionSpec as P

BF = jnp.bfloat16
F32 = jnp.float32
ANY = pl.BlockSpec(memory_space=pl.ANY)
VM = pl.BlockSpec(memory_space=pltpu.VMEM)
SM = pl.BlockSpec(memory_space=pltpu.SMEM)
MIB = 1024 * 1024
HBM = pl.BlockSpec(memory_space=pltpu.HBM)
TN = (((0,), (0,)), ((), ()))
NT = (((1,), (1,)), ((), ()))


def dot(a, b, dims=(((1,), (0,)), ((), ()))):
    return lax.dot_general(a, b, dims, preferred_element_type=F32)


def tree_steps(n_outer, n_inner):
    steps = []
    for name, size in (("outer", n_outer), ("inner", n_inner)):
        bit = 1
        while bit < size:
            steps.append((name, bit))
            bit *= 2
    return steps


def tree_offsets(steps):
    count = len(steps)
    table = []
    for slot in range(2**count):
        flip = {"outer": 0, "inner": 0}
        for k, (name, bit) in enumerate(steps):
            if (slot >> (count - 1 - k)) & 1:
                flip[name] ^= bit
        table.append((flip["outer"], flip["inner"]))
    return table


def hub_order(steps, n_inner, hd, nhubs):
    me = lax.axis_index("outer") * n_inner + lax.axis_index("inner")
    column = lax.broadcasted_iota(jnp.int32, (1, nhubs), 1)
    slot = column // hd
    flip = jnp.zeros((1, nhubs), jnp.int32)
    for k, (name, bit) in enumerate(steps):
        weight = bit * n_inner if name == "outer" else bit
        flip = flip + ((slot >> (len(steps) - 1 - k)) & 1) * weight
    target = (flip ^ me) * hd + column % hd
    row = lax.broadcasted_iota(jnp.int32, (nhubs, nhubs), 0)
    return (row == target).astype(F32).astype(BF)


def load_rows(ref, at, n):
    if n % 8 == 0:
        return ref[pl.ds(pl.multiple_of(at, n), n), :]
    return jnp.concatenate([ref[pl.ds(at + r, 1), :] for r in range(n)], axis=0)


def store_rows(ref, at, value):
    n = value.shape[0]
    if n % 8 == 0:
        ref[pl.ds(pl.multiple_of(at, n), n), :] = value
    else:
        for r in range(n):
            ref[pl.ds(at + r, 1), :] = value[r : r + 1, :]


def exchange(x, name, bit):
    size = lax.axis_size(name)
    return lax.ppermute(x, name, [(s, s ^ bit) for s in range(size)])


def direct_bits(steps):
    high, low = steps[-2][1], steps[-1][1]
    return [(high if c & 2 else 0) ^ (low if c & 1 else 0) for c in range(1, 4)]


def slot_onehot(rows_ref, count_ref, nrows, partners):
    slots = rows_ref.shape[1]
    sub = lax.broadcasted_iota(jnp.int32, (nrows, slots), 0)
    lane = lax.broadcasted_iota(jnp.int32, (1, slots), 1)
    parts = []
    for q in partners:
        live = jnp.where(lane < count_ref[0, q], rows_ref[pl.ds(q, 1), :], -1)
        parts.append((sub == live).astype(F32).astype(BF))
    return jnp.concatenate(parts, axis=1)


def gather_kernel(hub_ref, count_ref, feat_ref, rows_ref, out_ref, hub_out_ref):
    nrows, width = feat_ref.shape
    partners, slots = rows_ref.shape
    nhub = hub_ref.shape[0]
    feat = feat_ref[...]
    pick = slot_onehot(rows_ref, count_ref, nrows, range(partners))
    out_ref[...] = dot(pick, feat, TN).astype(BF).reshape(partners, slots, width)
    sub = lax.broadcasted_iota(jnp.int32, (16, nrows), 0)
    lane = lax.broadcasted_iota(jnp.int32, (16, nrows), 1)
    hot = jnp.zeros((16, nrows), F32)
    for h in range(nhub):
        hot = hot + ((sub == h) & (lane == hub_ref[h])).astype(F32)
    hub_out_ref[...] = dot(hot.astype(BF), feat)[:nhub].astype(BF)


def middle_kernel(
    steps,
    hub_steps,
    chunk,
    tile_src,
    feat_hbm,
    recv_hbm,
    hubx_hbm,
    adj_hbm,
    pre_hbm,
    wn_hbm,
    ws_hbm,
    cot_hbm,
    hidden_hbm,
    own_hbm,
    keep_hbm,
    give_hbm,
    *rest,
):
    n_inner = recv_hbm.shape[0]
    back_hbm, rest = rest[:n_inner], rest[n_inner:]
    (src, hubx, hubf, adj, pre0, wn, ws, cot, agg, hidden, gsrc, back, own, wacc, tail, tree, sems, osems) = rest
    o = lax.axis_index("outer")
    i = lax.axis_index("inner")
    offsets = tree_offsets(steps)
    nblocks, per_block = tile_src.shape
    tile = adj.shape[1]
    width = cot.shape[1]
    ntiles = src.shape[0]
    first_hub = nblocks + n_inner
    hd = hubx.shape[0] // len(offsets)
    pairs = [
        (hubx_hbm, hubx),
        (feat_hbm, src.at[pl.ds(0, nblocks)]),
        (recv_hbm, src.at[pl.ds(nblocks, n_inner)]),
        (adj_hbm, adj),
        (wn_hbm, wn),
        (pre_hbm, pre0),
        (cot_hbm, cot),
        (ws_hbm, ws),
    ]
    copies = [pltpu.make_async_copy(a, b, sems.at[k]) for k, (a, b) in enumerate(pairs)]
    for c in copies:
        c.start()
    half = keep_hbm.shape[0]
    outs = [
        pltpu.make_async_copy(hidden, hidden_hbm, osems.at[0]),
        pltpu.make_async_copy(own, own_hbm, osems.at[1]),
        pltpu.make_async_copy(tree.at[pl.ds(0, half)], keep_hbm, osems.at[2]),
        pltpu.make_async_copy(tree.at[pl.ds(half, half)], give_hbm, osems.at[3]),
    ]
    backs = [pltpu.make_async_copy(back.at[d], back_hbm[d], osems.at[4 + d]) for d in range(n_inner)]
    devices = [(o ^ fo) * n_inner + (i ^ fi) for fo, fi in offsets]
    gsrc[...] = jnp.zeros(gsrc.shape, F32)
    copies[0].wait()
    order = hub_order(hub_steps, n_inner, hd, hubx.shape[0])
    hubs = dot(order, hubx[...]).astype(BF)
    src[first_hub:] = hubs.reshape(ntiles - first_hub, tile, width)
    copies[1].wait()
    copies[2].wait()
    copies[3].wait()
    for b in range(nblocks):
        acc = jnp.zeros((tile, width), F32)
        for t in range(per_block):
            acc = acc + dot(adj[b * per_block + t], src[tile_src[b, t]])
        agg[b * tile : (b + 1) * tile, :] = acc.astype(BF)
    copies[4].wait()
    copies[5].wait()
    pre = pre0[...] + dot(agg[...], wn[...])
    copies[6].wait()
    sig = jax.nn.sigmoid(pre)
    hidden[...] = (pre * sig).astype(BF)
    outs[0].start()
    gp = (cot[...].astype(F32) * sig * (1.0 + pre * (1.0 - sig))).astype(BF)
    gagg = dot(gp, wn[...], NT).astype(BF)
    for b in range(nblocks):
        block = gagg[b * tile : (b + 1) * tile, :]
        for t in range(per_block):
            s = tile_src[b, t]
            gsrc[s] = gsrc[s] + dot(adj[b * per_block + t], block, TN)
    for d in range(n_inner):
        back[d] = gsrc[nblocks + (i ^ d)].astype(BF)
        backs[d].start()
    feat = src[0:nblocks].reshape(nblocks * tile, width)
    wacc[0:width, :] = dot(feat, gp, TN)
    wacc[width : 2 * width, :] = dot(agg[...], gp, TN)
    order = hub_order(steps, n_inner, hd, hubx.shape[0])
    hubf[...] = dot(order, gsrc[first_hub:].reshape(hubf.shape).astype(BF), TN)
    tail[...] = jnp.zeros(tail.shape, F32)
    tail[hd : hd + 1, :] = jnp.sum(gp.astype(F32), axis=0, keepdims=True)
    wrows = 2 * width // len(offsets)
    base = chunk - tail.shape[0]
    for j in reversed(range(len(devices))):
        d = devices[j]
        mine = load_rows(wacc, d * wrows, wrows)
        if base == wrows:
            tree[j * chunk : j * chunk + wrows, :] = mine.astype(BF)
        else:
            tail[8 : 8 + wrows, :] = mine
        tail[0:hd, :] = hubf[j * hd : (j + 1) * hd, :]
        tree[j * chunk + base : (j + 1) * chunk, :] = tail[...].astype(BF)
        if j * 2 == len(devices):
            outs[3].start()
    outs[2].start()
    copies[7].wait()
    own[...] = dot(gp, ws[...], NT) + gsrc[0:nblocks].reshape(own.shape)
    outs[1].start()
    for c in outs + backs:
        c.wait()


def scatter_kernel(base, hub_ref, count_ref, rows_ref, own_ref, part_ref, *rest):
    returned, (out_ref, acc) = rest[:-2], rest[-2:]
    nrows, width = own_ref.shape
    i = lax.axis_index("inner")
    acc[...] = own_ref[...]
    for d in range(0, len(returned), 2):
        put = slot_onehot(rows_ref, count_ref, nrows, (i ^ d, i ^ (d + 1)))
        acc[...] += dot(put, jnp.concatenate([returned[d][...], returned[d + 1][...]], axis=0))
    for h in range(hub_ref.shape[0]):
        r = hub_ref[h]
        acc[pl.ds(r, 1), :] = acc[pl.ds(r, 1), :] + part_ref[base + h : base + h + 1, :]
    out_ref[...] = acc[...].astype(BF)


def finish_kernel(steps, n_inner, factor, bias_row, x_ref, y_ref, part_ref, self_ref, neigh_ref, bias_ref, full):
    offsets = tree_offsets(steps)
    o = lax.axis_index("outer")
    i = lax.axis_index("inner")
    wrows = 2 * x_ref.shape[0] // len(offsets)
    width = self_ref.shape[0]
    for j, (fo, fi) in enumerate(offsets):
        d = (o ^ fo) * n_inner + (i ^ fi)
        ref, at = (x_ref, j) if 2 * j < len(offsets) else (y_ref, j - len(offsets) // 2)
        store_rows(full, d * wrows, ref[at * wrows : (at + 1) * wrows, :].astype(F32) * factor)
    self_ref[...] = full[0:width, :]
    neigh_ref[...] = full[width : 2 * width, :]
    bias_ref[...] = part_ref[bias_row : bias_row + 1, :] * factor


def params(mib):
    return pltpu.CompilerParams(vmem_limit_bytes=mib * MIB)


def nbytes(scratch):
    return sum(s.dtype.itemsize * math.prod(s.shape) for s in scratch)


def cost(flops, nbytes):
    return pl.CostEstimate(flops=flops, bytes_accessed=nbytes, transcendentals=0)


def body(
    features,
    adj_tiles,
    tile_src,
    send_rows,
    send_count,
    hub_rows,
    w_self,
    w_neigh,
    out_bias,
    cotangent,
):
    n_outer, n_inner = lax.axis_size("outer"), lax.axis_size("inner")
    ndevice = n_outer * n_inner
    nrows, width = features.shape
    tile = adj_tiles.shape[1]
    nblocks, per_block = tile_src.shape
    hd = hub_rows.shape[0]
    nhubs = hd * ndevice
    ntiles = nblocks + n_inner + nhubs // tile
    steps = tree_steps(n_outer, n_inner)
    offsets = tree_offsets(steps)
    wrows = 2 * width // ndevice
    chunk = wrows + 16 if wrows % 16 == 0 else 16
    base = chunk - 16

    outgoing, hub_own = pl.pallas_call(
        gather_kernel,
        out_shape=(
            jax.ShapeDtypeStruct((n_inner, tile, width), BF),
            jax.ShapeDtypeStruct((hd, width), BF),
        ),
        in_specs=[SM, SM, VM, VM],
        out_specs=(VM, VM),
        compiler_params=params(60),
        cost_estimate=cost(4 * 10**8, 3 * 10**6),
        name="gather_rows",
    )(hub_rows, send_count, features, send_rows)
    received = lax.all_to_all(outgoing, "inner", split_axis=0, concat_axis=0, tiled=True)
    hubx = hub_own
    for name, bit in steps[:-2]:
        hubx = lax.optimization_barrier(jnp.concatenate([hubx, exchange(hubx, name, bit)], 0))
    hubx = jnp.concatenate([hubx] + [exchange(hubx, "inner", bit) for bit in direct_bits(steps)], 0)
    hub_steps = steps[-2:] + steps[:-2][::-1]
    self_low = w_self.astype(BF)
    neigh_low = w_neigh.astype(BF)
    pre0 = jnp.dot(features, self_low, preferred_element_type=F32) + out_bias

    half = ndevice * chunk // 2
    scratch = [
        pltpu.VMEM((ntiles, tile, width), BF),
        pltpu.VMEM((nhubs, width), BF),
        pltpu.VMEM((nhubs, width), F32),
        pltpu.VMEM(adj_tiles.shape, BF),
        pltpu.VMEM((nrows, width), F32),
        pltpu.VMEM((width, width), BF),
        pltpu.VMEM((width, width), BF),
        pltpu.VMEM((nrows, width), BF),
        pltpu.VMEM((nrows, width), BF),
        pltpu.VMEM((nrows, width), BF),
        pltpu.VMEM((ntiles, tile, width), F32),
        pltpu.VMEM((n_inner, tile, width), BF),
        pltpu.VMEM((nrows, width), F32),
        pltpu.VMEM((2 * width, width), F32),
        pltpu.VMEM((16, width), F32),
        pltpu.VMEM((ndevice * chunk, width), BF),
    ]
    hidden_out, own, keep, give, *back = pl.pallas_call(
        functools.partial(middle_kernel, steps, hub_steps, chunk),
        out_shape=(
            jax.ShapeDtypeStruct((nrows, width), BF),
            jax.ShapeDtypeStruct((nrows, width), F32),
            jax.ShapeDtypeStruct((half, width), BF),
            jax.ShapeDtypeStruct((half, width), BF),
        )
        + (jax.ShapeDtypeStruct((tile, width), BF),) * n_inner,
        in_specs=[SM, HBM, ANY, ANY, HBM, ANY, ANY, ANY, HBM],
        out_specs=(ANY,) * (4 + n_inner),
        scratch_shapes=scratch
        + [
            pltpu.SemaphoreType.DMA((8,)),
            pltpu.SemaphoreType.DMA((4 + n_inner,)),
        ],
        compiler_params=params(nbytes(scratch) // MIB + 12),
        cost_estimate=cost(2 * 10**9, 9 * 10**6),
        name="middle",
    )(
        tile_src,
        features.reshape(nblocks, tile, width),
        received,
        hubx,
        adj_tiles,
        pre0,
        neigh_low,
        self_low,
        cotangent,
    )
    returned = [back[0]] + [None] * (n_inner - 1)
    far = n_inner // 2

    def start(ds, held):
        for d, value in zip(ds, held):
            returned[d] = exchange(value, "inner", d)

    def after(value, ds):
        value, held = lax.optimization_barrier((value, [returned[d] for d in ds]))
        for d, block in zip(ds, held):
            returned[d] = block
        return value

    first, second = list(range(far, n_inner - 2)), [n_inner - 2]
    third, fourth = [n_inner - 1], list(range(1, far))
    start(first + second, [back[d] for d in first + second])
    got = exchange(give, *steps[0])
    part = keep.astype(F32) + got.astype(F32)
    for k, (name, bit) in enumerate(steps[1:-2]):
        rows = part.shape[0] // 2
        send = part[rows:].astype(BF)
        if k == len(steps) - 4:
            send = after(send, first)
        part = part[:rows] + exchange(send, name, bit).astype(F32)
    quarter = part.shape[0] // 4
    pieces = [part[c * quarter : (c + 1) * quarter].astype(BF) for c in range(1, 4)]
    pieces = after(pieces, second)
    part = part[:quarter]
    for bit, piece in zip(direct_bits(steps), pieces):
        part = part + exchange(piece, "inner", bit).astype(F32)
    at = 0 if wrows % 16 == 0 else 8
    mine = part[at : at + wrows].astype(BF)
    parts = [mine] + [exchange(mine, "inner", bit) for bit in direct_bits(steps)]
    gathered = jnp.concatenate(parts, 0)
    gathered, held = lax.optimization_barrier((gathered, [back[d] for d in third + fourth]))
    start(third + fourth, held)
    for k, (name, bit) in enumerate(reversed(steps[1:-2])):
        if k == 1:
            gathered = after(gathered, third)
        gathered = lax.optimization_barrier(jnp.concatenate([gathered, exchange(gathered, name, bit)], 0))
    gathered = after(gathered, fourth)
    other = exchange(gathered, *steps[0])

    grad_features = pl.pallas_call(
        functools.partial(scatter_kernel, base),
        out_shape=jax.ShapeDtypeStruct((nrows, width), BF),
        in_specs=[SM, SM] + [VM] * (3 + n_inner),
        out_specs=VM,
        scratch_shapes=[pltpu.VMEM((nrows, width), F32)],
        compiler_params=params(24),
        cost_estimate=cost(4 * 10**8, 3 * 10**6),
        name="scatter_rows",
    )(hub_rows, send_count, send_rows, own, part, *returned)
    factor = 1.0 / float(nrows * ndevice) ** 0.5
    total_self, total_neigh, total_bias = pl.pallas_call(
        functools.partial(finish_kernel, steps, n_inner, factor, base + hd),
        out_shape=(jax.ShapeDtypeStruct((width, width), F32),) * 2 + (jax.ShapeDtypeStruct((1, width), F32),),
        in_specs=[VM] * 3,
        out_specs=(VM,) * 3,
        scratch_shapes=[pltpu.VMEM((2 * width, width), F32)],
        compiler_params=params(24),
        cost_estimate=cost(10**6, 3 * 10**6),
        name="finish",
    )(gathered, other, part)
    return hidden_out, grad_features, total_self, total_neigh, total_bias.reshape(width)


def solution(mesh):
    both = ("outer", "inner")
    return jax.shard_map(
        body,
        mesh=mesh,
        in_specs=(
            P(both, None),
            P(both, None, None),
            P(both, None),
            P(both, None),
            P(both, None),
            P(both),
            P(),
            P(),
            P(),
            P(both, None),
        ),
        out_specs=(P(both, None), P(both, None), P(), P(), P()),
        check_vma=False,
    )
```

```python
import functools
import math

import jax
import jax.numpy as jnp
from jax import lax
from jax.experimental import pallas as pl
from jax.experimental.pallas import tpu as pltpu
from jax.sharding import PartitionSpec as P

BF = jnp.bfloat16
F32 = jnp.float32
VM = pl.BlockSpec(memory_space=pltpu.VMEM)
SM = pl.BlockSpec(memory_space=pltpu.SMEM)
MIB = 1024 * 1024
TN = (((0,), (0,)), ((), ()))
NT = (((1,), (1,)), ((), ()))


def dot(a, b, dims=(((1,), (0,)), ((), ()))):
    return lax.dot_general(a, b, dims, preferred_element_type=F32)


def tree_groups(n_outer, n_inner):
    steps = []
    bit = 1
    while bit < n_outer:
        steps.append((bit, 0))
        bit *= 2
    bit = 1
    while bit < n_inner:
        steps.append((0, bit))
        bit *= 2
    middle = steps[1:-2]
    return [steps[:1]] + [middle[k : k + 2] for k in range(0, len(middle), 2)] + [steps[-2:]]


def flips(steps):
    count = len(steps)
    table = []
    for slot in range(2**count):
        fo = fi = 0
        for k, (bo, bi) in enumerate(steps):
            if (slot >> (count - 1 - k)) & 1:
                fo, fi = fo ^ bo, fi ^ bi
        table.append((fo, fi))
    return table


def hub_order(steps, n_inner, hd, nhubs):
    me = lax.axis_index("outer") * n_inner + lax.axis_index("inner")
    column = lax.broadcasted_iota(jnp.int32, (1, nhubs), 1)
    slot = column // hd
    flip = jnp.zeros((1, nhubs), jnp.int32)
    for k, (bo, bi) in enumerate(steps):
        flip = flip + ((slot >> (len(steps) - 1 - k)) & 1) * (bo * n_inner + bi)
    target = (flip ^ me) * hd + column % hd
    row = lax.broadcasted_iota(jnp.int32, (nhubs, nhubs), 0)
    return (row == target).astype(F32).astype(BF)


def load_rows(ref, at, n):
    if n % 8 == 0:
        return ref[pl.ds(pl.multiple_of(at, n), n), :]
    return jnp.concatenate([ref[pl.ds(at + r, 1), :] for r in range(n)], axis=0)


def store_rows(ref, at, value):
    n = value.shape[0]
    if n % 8 == 0:
        ref[pl.ds(pl.multiple_of(at, n), n), :] = value
    else:
        for r in range(n):
            ref[pl.ds(at + r, 1), :] = value[r : r + 1, :]


def exchange(x, flip):
    n_outer, n_inner = lax.axis_size("outer"), lax.axis_size("inner")
    mask = flip[0] * n_inner + flip[1]
    return lax.ppermute(x, ("outer", "inner"), [(s, s ^ mask) for s in range(n_outer * n_inner)])


def spread(x, group):
    parts = [x] + [exchange(x, flip) for flip in flips(group)[1:]]
    return lax.optimization_barrier(jnp.concatenate(parts, 0))


def slot_onehot(rows_ref, count_ref, nrows, partners):
    slots = rows_ref.shape[1]
    sub = lax.broadcasted_iota(jnp.int32, (nrows, slots), 0)
    lane = lax.broadcasted_iota(jnp.int32, (1, slots), 1)
    parts = []
    for q in partners:
        live = jnp.where(lane < count_ref[0, q], rows_ref[pl.ds(q, 1), :], -1)
        parts.append((sub == live).astype(F32).astype(BF))
    return jnp.concatenate(parts, axis=1)


def gather_kernel(hub_ref, count_ref, feat_ref, rows_ref, hub_out_ref, *outs):
    nrows = feat_ref.shape[0]
    slots = rows_ref.shape[1]
    nhub = hub_ref.shape[0]
    i = lax.axis_index("inner")
    feat = feat_ref[...]
    sub = lax.broadcasted_iota(jnp.int32, (16, nrows), 0)
    lane = lax.broadcasted_iota(jnp.int32, (16, nrows), 1)
    hot = jnp.zeros((16, nrows), F32)
    for h in range(nhub):
        hot = hot + ((sub == h) & (lane == hub_ref[h])).astype(F32)
    hub_out_ref[...] = dot(hot.astype(BF), feat)[:nhub].astype(BF)
    pick = slot_onehot(rows_ref, count_ref, nrows, [i ^ d for d in range(len(outs))])
    rows = dot(pick, feat, TN).astype(BF)
    for d, out in enumerate(outs):
        out[...] = rows[d * slots : (d + 1) * slots, :]


def prepare_kernel(feat_ref, adj_ref, wn_ref, cot_ref, feat_t, adj_cat, adj_t, wn_low, wn_t, cot_wide):
    feat_t[...] = feat_ref[...].T
    nblocks, tile, _ = adj_cat.shape
    per_block = adj_ref.shape[0] // nblocks
    for b in range(nblocks):
        for t in range(per_block):
            block = adj_ref[b * per_block + t]
            adj_cat[b, :, t * tile : (t + 1) * tile] = block
            adj_t[b, t * tile : (t + 1) * tile, :] = block.T
    low = wn_ref[...].astype(BF)
    wn_low[...] = low
    wn_t[...] = low.T
    cot_wide[...] = cot_ref[...].astype(F32)


def middle_kernel(
    steps,
    hub_steps,
    tile_src,
    feat,
    feat_t,
    hubx,
    adj_cat,
    adj_t,
    pre0,
    wn,
    wn_t,
    cot,
    *rest,
):
    n_inner = (len(rest) - 11) // 2
    recv, (pre_out, gp_out, gown, keep, give), rest = rest[:n_inner], rest[n_inner : n_inner + 5], rest[n_inner + 5 :]
    back, (src, agg, gsrc, wacc, wperm, hubf) = rest[:n_inner], rest[n_inner:]
    o = lax.axis_index("outer")
    i = lax.axis_index("inner")
    table = flips(steps)
    nblocks, per_block = tile_src.shape
    tile = adj_cat.shape[1]
    nrows, width = cot.shape
    ntiles = src.shape[0]
    first_hub = nblocks + n_inner
    nhubs = hubx.shape[0]
    hd = nhubs // len(table)
    src[0:nblocks] = feat[...]
    for d in range(n_inner):
        src[nblocks + (i ^ d)] = recv[d][...]
    order = hub_order(hub_steps, n_inner, hd, nhubs)
    src[first_hub:] = dot(order, hubx[...]).astype(BF).reshape(ntiles - first_hub, tile, width)
    for b in range(nblocks):
        acc = jnp.zeros((tile, width), F32)
        for t in range(0, per_block, 2):
            ts = range(t, min(t + 2, per_block))
            rhs = [src[tile_src[b, u]] for u in ts]
            rhs = rhs[0] if len(rhs) == 1 else jnp.concatenate(rhs, axis=0)
            acc = acc + dot(adj_cat[b, :, t * tile : (t + len(ts)) * tile], rhs)
        agg[b * tile : (b + 1) * tile, :] = acc.astype(BF)
    pre = pre0[...] + dot(agg[...], wn[...])
    pre_out[...] = pre
    sig = jax.nn.sigmoid(pre)
    gp = (cot[...] * sig * (1.0 + pre * (1.0 - sig))).astype(BF)
    gp_out[...] = gp
    gagg = dot(gp, wn_t[...]).astype(BF)
    gsrc[...] = jnp.zeros(gsrc.shape, F32)
    for b in range(nblocks):
        for t in range(0, per_block, 3):
            last = min(t + 3, per_block)
            some = dot(adj_t[b, t * tile : last * tile, :], gagg[b * tile : (b + 1) * tile, :])
            for u in range(t, last):
                s = tile_src[b, u]
                gsrc[s] = gsrc[s] + some[(u - t) * tile : (u - t + 1) * tile, :]
    for d in range(n_inner):
        back[d][...] = gsrc[nblocks + (i ^ d)].astype(BF)
    gown[...] = gsrc[0:nblocks].reshape(nrows, width)
    wacc[0:width, :] = dot(feat_t[...], gp)
    wacc[width : 2 * width, :] = dot(agg[...], gp, TN)
    order = hub_order(steps, n_inner, hd, nhubs)
    hubf[...] = dot(order, gsrc[first_hub:].reshape(nhubs, width).astype(BF), TN).astype(BF)
    bias = jnp.sum(gp.astype(F32), axis=0, keepdims=True)
    tail = jnp.where(lax.broadcasted_iota(jnp.int32, (16, width), 0) == 0, bias, 0.0).astype(BF)
    wrows = 2 * width // len(table)
    devices = [(o ^ fo) * n_inner + (i ^ fi) for fo, fi in table]
    for k, out in enumerate((keep, give)):
        for j in range(len(table) // 2):
            rows = load_rows(wacc, devices[k * len(table) // 2 + j] * wrows, wrows)
            if wrows % 16 == 0:
                out[j * wrows : (j + 1) * wrows, :] = rows.astype(BF)
            else:
                wperm[j * wrows : (j + 1) * wrows, :] = rows
        if wrows % 16:
            out[0:width, :] = wperm[...].astype(BF)
        out[width : width + nhubs // 2, :] = hubf[k * nhubs // 2 : (k + 1) * nhubs // 2, :]
        out[width + nhubs // 2 :, :] = tail


def add_returned(acc, rows_ref, count_ref, blocks, returned):
    i = lax.axis_index("inner")
    for k in range(0, len(blocks), 2):
        some = range(k, min(k + 2, len(blocks)))
        put = slot_onehot(rows_ref, count_ref, acc.shape[0], [i ^ blocks[u] for u in some])
        values = [returned[u][...] for u in some]
        acc[...] += dot(put, values[0] if len(values) == 1 else jnp.concatenate(values, axis=0))


def first_scatter_kernel(blocks, count_ref, rows_ref, gown_ref, gp_ref, ws_ref, *rest):
    returned, out_ref = rest[:-1], rest[-1]
    out_ref[...] = gown_ref[...] + dot(gp_ref[...], ws_ref[...], NT)
    add_returned(out_ref, rows_ref, count_ref, blocks, returned)


def last_scatter_kernel(blocks, hub_ref, count_ref, rows_ref, own_ref, hub_grad_ref, *rest):
    returned, (out_ref, acc) = rest[:-2], rest[-2:]
    acc[...] = own_ref[...]
    add_returned(acc, rows_ref, count_ref, blocks, returned)
    for h in range(hub_ref.shape[0]):
        r = hub_ref[h]
        acc[pl.ds(r, 1), :] = acc[pl.ds(r, 1), :] + hub_grad_ref[h : h + 1, :]
    out_ref[...] = acc[...].astype(BF)


def finish_kernel(steps, n_inner, factor, x_ref, y_ref, bias_in, self_ref, neigh_ref, bias_ref, full):
    table = flips(steps)
    o = lax.axis_index("outer")
    i = lax.axis_index("inner")
    wrows = 2 * x_ref.shape[0] // len(table)
    width = self_ref.shape[0]
    for j, (fo, fi) in enumerate(table):
        d = (o ^ fo) * n_inner + (i ^ fi)
        ref, at = (x_ref, j) if 2 * j < len(table) else (y_ref, j - len(table) // 2)
        store_rows(full, d * wrows, ref[at * wrows : (at + 1) * wrows, :].astype(F32) * factor)
    self_ref[...] = full[0:width, :]
    neigh_ref[...] = full[width : 2 * width, :]
    bias_ref[...] = bias_in[0:1, :] * factor


def params(mib):
    return pltpu.CompilerParams(vmem_limit_bytes=mib * MIB)


def nbytes(scratch):
    return sum(s.dtype.itemsize * math.prod(s.shape) for s in scratch)


def cost(flops, nbytes):
    return pl.CostEstimate(flops=flops, bytes_accessed=nbytes, transcendentals=0)


def body(
    features,
    adj_tiles,
    tile_src,
    send_rows,
    send_count,
    hub_rows,
    w_self,
    w_neigh,
    out_bias,
    cotangent,
):
    n_outer, n_inner = lax.axis_size("outer"), lax.axis_size("inner")
    ndevice = n_outer * n_inner
    nrows, width = features.shape
    tile = adj_tiles.shape[1]
    nblocks, per_block = tile_src.shape
    hd = hub_rows.shape[0]
    nhubs = hd * ndevice
    ntiles = nblocks + n_inner + nhubs // tile
    groups = tree_groups(n_outer, n_inner)
    steps = sum(groups, [])
    hub_steps = sum(groups[::-1], [])
    wrows = 2 * width // ndevice

    def shape(*dims, dtype=BF):
        return jax.ShapeDtypeStruct(dims, dtype)

    hub_own, *outgoing = pl.pallas_call(
        gather_kernel,
        out_shape=(shape(hd, width),) + (shape(tile, width),) * n_inner,
        in_specs=[SM, SM, VM, VM],
        out_specs=(VM,) * (1 + n_inner),
        compiler_params=params(60),
        cost_estimate=cost(4 * 10**8, 3 * 10**6),
        name="gather_rows",
    )(hub_rows, send_count, features, send_rows)
    received = [outgoing[0]] + [None] * (n_inner - 1)
    for d in range(1, n_inner):
        received[d] = exchange(outgoing[d], (0, d))
    far = n_inner // 2
    hubx = hub_own
    for group in groups[:-1]:
        hubx = spread(hubx, group)
    ahead = range(far, far + far // 2)
    hubx, held = lax.optimization_barrier((hubx, [received[d] for d in ahead]))
    for d, value in zip(ahead, held):
        received[d] = value
    hubx = spread(hubx, groups[-1])
    feat_t, adj_cat, adj_t, neigh_low, neigh_t, cot_wide = pl.pallas_call(
        prepare_kernel,
        out_shape=(
            shape(width, nrows),
            shape(nblocks, tile, per_block * tile),
            shape(nblocks, per_block * tile, tile),
            shape(width, width),
            shape(width, width),
            shape(nrows, width, dtype=F32),
        ),
        in_specs=[VM] * 4,
        out_specs=(VM,) * 6,
        compiler_params=params(8 + 4 * nbytes([adj_tiles]) // MIB),
        cost_estimate=cost(10**6, 7 * 10**6),
        name="prepare",
    )(features, adj_tiles, w_neigh, cotangent)
    self_low = w_self.astype(BF)
    pre0 = jnp.dot(features, self_low, preferred_element_type=F32) + out_bias

    half = width + nhubs // 2 + 16
    scratch = [
        pltpu.VMEM((ntiles, tile, width), BF),
        pltpu.VMEM((nrows, width), BF),
        pltpu.VMEM((ntiles, tile, width), F32),
        pltpu.VMEM((2 * width, width), F32),
        pltpu.VMEM((width, width) if wrows % 16 else (8, 128), F32),
        pltpu.VMEM((nhubs, width), BF),
    ]
    out_shape = (
        shape(nrows, width, dtype=F32),
        shape(nrows, width),
        shape(nrows, width, dtype=F32),
        shape(half, width),
        shape(half, width),
    ) + (shape(tile, width),) * n_inner
    operands = (
        features.reshape(nblocks, tile, width),
        feat_t,
        hubx,
        adj_cat,
        adj_t,
        pre0,
        neigh_low,
        neigh_t,
        cot_wide,
        *received,
    )
    pre, gp, gown, keep, give, *back = pl.pallas_call(
        functools.partial(middle_kernel, steps, hub_steps),
        out_shape=out_shape,
        in_specs=[SM] + [VM] * len(operands),
        out_specs=(VM,) * len(out_shape),
        scratch_shapes=scratch,
        compiler_params=params(nbytes([*scratch, *operands, *out_shape]) // MIB + 8),
        cost_estimate=cost(2 * 10**9, 9 * 10**6),
        name="middle",
    )(tile_src, *operands)
    hidden_out = (pre * jax.nn.sigmoid(pre)).astype(BF)

    returned = [back[0]] + [None] * (n_inner - 1)
    odd = list(range(far + 1, n_inner, 2))
    first = list(range(far, n_inner, 2))
    second = [1] + odd[: far // 4]
    third = [3] + odd[far // 4 :]
    fourth = [d for d in range(2, far) if d != 3]

    def start(ds, after=None):
        held = [back[d] for d in ds]
        if after is not None:
            after, held = lax.optimization_barrier((after, held))
        for d, value in zip(ds, held):
            returned[d] = exchange(value, (0, d))
        return after

    def wait(value, ds):
        value, held = lax.optimization_barrier((value, [returned[d] for d in ds]))
        for d, block in zip(ds, held):
            returned[d] = block
        return value

    def reduce(parts, group, pending=()):
        ways = 2 ** len(group)
        seg = [p.shape[0] // ways for p in parts[:2]]
        sends = []
        for c in range(1, ways):
            rows = [p[c * n : (c + 1) * n] for p, n in zip(parts, seg)]
            sends.append(jnp.concatenate(rows + [parts[2]], 0).astype(BF))
        if pending:
            sends = wait(sends, pending)
        w, hub, bias = parts[0][: seg[0]], parts[1][: seg[1]], parts[2]
        for flip, send in zip(flips(group)[1:], sends):
            got = exchange(send, flip).astype(F32)
            w, hub, bias = w + got[: seg[0]], hub + got[seg[0] : seg[0] + seg[1]], bias + got[seg[0] + seg[1] :]
        return w, hub, bias

    start(first)
    got = exchange(give, flips(groups[0])[1])
    part = keep.astype(F32) + got.astype(F32)
    parts = (part[:width], part[width : width + nhubs // 2], part[width + nhubs // 2 : width + nhubs // 2 + 8])
    for group in groups[1:-1]:
        parts = reduce(parts, group)
    parts = start(second, parts)
    part, hub_grad, bias_sum = reduce(parts, groups[-1])
    mine = wait(part.astype(BF), first)
    mine, hidden_out = lax.optimization_barrier((mine, hidden_out))
    mine = start(third, mine)
    gathered = spread(mine, groups[-1])
    gathered = start(fourth, gathered)
    gathered = wait(gathered, second)
    for group in groups[1:-1][::-1]:
        gathered = spread(gathered, group)
    gathered = wait(gathered, third + fourth)

    blocks = [0] + first + second
    own = pl.pallas_call(
        functools.partial(first_scatter_kernel, blocks),
        out_shape=shape(nrows, width, dtype=F32),
        in_specs=[SM] + [VM] * (4 + len(blocks)),
        out_specs=VM,
        compiler_params=params(16),
        cost_estimate=cost(4 * 10**8, 3 * 10**6),
        name="scatter_first",
    )(send_count, send_rows, gown, gp, self_low, *[returned[d] for d in blocks])
    gathered, own = lax.optimization_barrier((gathered, own))
    other = exchange(gathered, flips(groups[0])[1])
    blocks = third + fourth
    grad_features = pl.pallas_call(
        functools.partial(last_scatter_kernel, blocks),
        out_shape=shape(nrows, width),
        in_specs=[SM, SM] + [VM] * (3 + len(blocks)),
        out_specs=VM,
        scratch_shapes=[pltpu.VMEM((nrows, width), F32)],
        compiler_params=params(16),
        cost_estimate=cost(2 * 10**8, 2 * 10**6),
        name="scatter_last",
    )(hub_rows, send_count, send_rows, own, hub_grad, *[returned[d] for d in blocks])
    factor = 1.0 / float(nrows * ndevice) ** 0.5
    total_self, total_neigh, total_bias = pl.pallas_call(
        functools.partial(finish_kernel, steps, n_inner, factor),
        out_shape=(shape(width, width, dtype=F32),) * 2 + (shape(1, width, dtype=F32),),
        in_specs=[VM] * 3,
        out_specs=(VM,) * 3,
        scratch_shapes=[pltpu.VMEM((2 * width, width), F32)],
        compiler_params=params(16),
        cost_estimate=cost(10**6, 3 * 10**6),
        name="finish",
    )(gathered, other, bias_sum)
    return hidden_out, grad_features, total_self, total_neigh, total_bias.reshape(width)


def solution(mesh):
    both = ("outer", "inner")
    return jax.shard_map(
        body,
        mesh=mesh,
        in_specs=(
            P(both, None),
            P(both, None, None),
            P(both, None),
            P(both, None),
            P(both, None),
            P(both),
            P(),
            P(),
            P(),
            P(both, None),
        ),
        out_specs=(P(both, None), P(both, None), P(), P(), P()),
        check_vma=False,
    )
```

```python
import functools
import math

import jax
import jax.numpy as jnp
from jax import lax
from jax.experimental import pallas as pl
from jax.experimental.pallas import tpu as pltpu
from jax.sharding import PartitionSpec as P

BF = jnp.bfloat16
F32 = jnp.float32
VM = pl.BlockSpec(memory_space=pltpu.VMEM)
SM = pl.BlockSpec(memory_space=pltpu.SMEM)
MIB = 1024 * 1024
TN = (((0,), (0,)), ((), ()))
NT = (((1,), (1,)), ((), ()))


def dot(a, b, dims=(((1,), (0,)), ((), ()))):
    return lax.dot_general(a, b, dims, preferred_element_type=F32)


def tree_groups(n_outer, n_inner):
    steps = []
    bit = 1
    while bit < n_outer:
        steps.append((bit, 0))
        bit *= 2
    bit = 1
    while bit < n_inner:
        steps.append((0, bit))
        bit *= 2
    middle = steps[1:-2]
    return [steps[:1]] + [middle[k : k + 2] for k in range(0, len(middle), 2)] + [steps[-2:]]


def flips(steps):
    count = len(steps)
    table = []
    for slot in range(2**count):
        fo = fi = 0
        for k, (bo, bi) in enumerate(steps):
            if (slot >> (count - 1 - k)) & 1:
                fo, fi = fo ^ bo, fi ^ bi
        table.append((fo, fi))
    return table


def hub_order(steps, n_inner, hd, nhubs):
    me = lax.axis_index("outer") * n_inner + lax.axis_index("inner")
    column = lax.broadcasted_iota(jnp.int32, (1, nhubs), 1)
    slot = column // hd
    flip = jnp.zeros((1, nhubs), jnp.int32)
    for k, (bo, bi) in enumerate(steps):
        flip = flip + ((slot >> (len(steps) - 1 - k)) & 1) * (bo * n_inner + bi)
    target = (flip ^ me) * hd + column % hd
    row = lax.broadcasted_iota(jnp.int32, (nhubs, nhubs), 0)
    return (row == target).astype(F32).astype(BF)


def load_rows(ref, at, n):
    if n % 8 == 0:
        return ref[pl.ds(pl.multiple_of(at, n), n), :]
    return jnp.concatenate([ref[pl.ds(at + r, 1), :] for r in range(n)], axis=0)


def store_rows(ref, at, value):
    n = value.shape[0]
    if n % 8 == 0:
        ref[pl.ds(pl.multiple_of(at, n), n), :] = value
    else:
        for r in range(n):
            ref[pl.ds(at + r, 1), :] = value[r : r + 1, :]


def exchange(x, flip):
    n_outer, n_inner = lax.axis_size("outer"), lax.axis_size("inner")
    mask = flip[0] * n_inner + flip[1]
    return lax.ppermute(x, ("outer", "inner"), [(s, s ^ mask) for s in range(n_outer * n_inner)])


def spread(x, group):
    parts = [x] + [exchange(x, flip) for flip in flips(group)[1:]]
    return lax.optimization_barrier(jnp.concatenate(parts, 0))


def relayed(n_inner):
    return list(range(2, n_inner - 2, 2))


def places(n_inner, tile):
    pairs = relayed(n_inner)
    near = 1 + len(pairs)
    where = {0: (0, 0), 1: (near, 0), n_inner - 2: (near + 1, 0), n_inner - 1: (near + 2, 0)}
    for k, c in enumerate(pairs):
        where[c] = (1 + k, 0)
        where[c + 1] = (near, (1 + k) * tile)
    return where


def sent_blocks(n_inner):
    return [[0]] + [[c, c + 1] for c in relayed(n_inner)] + [[1], [n_inner - 2], [n_inner - 1]]


def relay(pairs, one):
    rows = one.shape[0]
    return exchange(jnp.concatenate([one] + [p[rows:] for p in pairs], 0), (0, 1))


def slot_onehot(rows_ref, count_ref, nrows, partners):
    slots = rows_ref.shape[1]
    sub = lax.broadcasted_iota(jnp.int32, (nrows, slots), 0)
    lane = lax.broadcasted_iota(jnp.int32, (1, slots), 1)
    parts = []
    for q in partners:
        live = jnp.where(lane < count_ref[0, q], rows_ref[pl.ds(q, 1), :], -1)
        parts.append((sub == live).astype(F32).astype(BF))
    return jnp.concatenate(parts, axis=1)


def gather_kernel(hub_ref, count_ref, feat_ref, rows_ref, hub_out_ref, *outs):
    nrows = feat_ref.shape[0]
    n_inner, slots = rows_ref.shape
    nhub = hub_ref.shape[0]
    i = lax.axis_index("inner")
    feat = feat_ref[...]
    sub = lax.broadcasted_iota(jnp.int32, (16, nrows), 0)
    lane = lax.broadcasted_iota(jnp.int32, (16, nrows), 1)
    hot = jnp.zeros((16, nrows), F32)
    for h in range(nhub):
        hot = hot + ((sub == h) & (lane == hub_ref[h])).astype(F32)
    hub_out_ref[...] = dot(hot.astype(BF), feat)[:nhub].astype(BF)
    blocks = sent_blocks(n_inner)
    order = [d for some in blocks for d in some]
    pick = slot_onehot(rows_ref, count_ref, nrows, [i ^ d for d in order])
    rows = dot(pick, feat, TN).astype(BF)
    at = 0
    for some, out in zip(blocks, outs):
        out[...] = rows[at * slots : (at + len(some)) * slots, :]
        at += len(some)


def prepare_kernel(feat_ref, adj_ref, wn_ref, cot_ref, feat_t, adj_cat, adj_t, wn_low, wn_t, cot_wide):
    feat_t[...] = feat_ref[...].T
    nblocks, tile, _ = adj_cat.shape
    per_block = adj_ref.shape[0] // nblocks
    for b in range(nblocks):
        for t in range(per_block):
            block = adj_ref[b * per_block + t]
            adj_cat[b, :, t * tile : (t + 1) * tile] = block
            adj_t[b, t * tile : (t + 1) * tile, :] = block.T
    low = wn_ref[...].astype(BF)
    wn_low[...] = low
    wn_t[...] = low.T
    cot_wide[...] = cot_ref[...].astype(F32)


def middle_kernel(
    steps,
    hub_steps,
    n_inner,
    tile_src,
    feat,
    feat_t,
    hubx,
    adj_cat,
    adj_t,
    pre0,
    wn,
    wn_t,
    cot,
    *rest,
):
    count = (len(rest) - 11) // 2
    recv, (pre_out, gp_out, gown, keep, give), rest = rest[:count], rest[count : count + 5], rest[count + 5 :]
    back, (src, agg, gsrc, wacc, wperm, hubf) = rest[:count], rest[count:]
    o = lax.axis_index("outer")
    i = lax.axis_index("inner")
    table = flips(steps)
    nblocks, per_block = tile_src.shape
    tile = adj_cat.shape[1]
    nrows, width = cot.shape
    ntiles = src.shape[0]
    first_hub = nblocks + n_inner
    nhubs = hubx.shape[0]
    hd = nhubs // len(table)
    src[0:nblocks] = feat[...]
    for d, (k, at) in places(n_inner, tile).items():
        src[nblocks + (i ^ d)] = recv[k][at : at + tile, :]
    order = hub_order(hub_steps, n_inner, hd, nhubs)
    src[first_hub:] = dot(order, hubx[...]).astype(BF).reshape(ntiles - first_hub, tile, width)
    for b in range(nblocks):
        acc = jnp.zeros((tile, width), F32)
        for t in range(0, per_block, 2):
            ts = range(t, min(t + 2, per_block))
            rhs = [src[tile_src[b, u]] for u in ts]
            rhs = rhs[0] if len(rhs) == 1 else jnp.concatenate(rhs, axis=0)
            acc = acc + dot(adj_cat[b, :, t * tile : (t + len(ts)) * tile], rhs)
        agg[b * tile : (b + 1) * tile, :] = acc.astype(BF)
    pre = pre0[...] + dot(agg[...], wn[...])
    pre_out[...] = pre
    sig = jax.nn.sigmoid(pre)
    gp = (cot[...] * sig * (1.0 + pre * (1.0 - sig))).astype(BF)
    gp_out[...] = gp
    gagg = dot(gp, wn_t[...]).astype(BF)
    gsrc[...] = jnp.zeros(gsrc.shape, F32)
    for b in range(nblocks):
        for t in range(0, per_block, 3):
            last = min(t + 3, per_block)
            some = dot(adj_t[b, t * tile : last * tile, :], gagg[b * tile : (b + 1) * tile, :])
            for u in range(t, last):
                s = tile_src[b, u]
                gsrc[s] = gsrc[s] + some[(u - t) * tile : (u - t + 1) * tile, :]
    for some, out in zip(sent_blocks(n_inner), back):
        for k, d in enumerate(some):
            out[k * tile : (k + 1) * tile, :] = gsrc[nblocks + (i ^ d)].astype(BF)
    gown[...] = gsrc[0:nblocks].reshape(nrows, width)
    wacc[0:width, :] = dot(feat_t[...], gp)
    wacc[width : 2 * width, :] = dot(agg[...], gp, TN)
    order = hub_order(steps, n_inner, hd, nhubs)
    hubf[...] = dot(order, gsrc[first_hub:].reshape(nhubs, width).astype(BF), TN).astype(BF)
    bias = jnp.sum(gp.astype(F32), axis=0, keepdims=True)
    tail = jnp.where(lax.broadcasted_iota(jnp.int32, (16, width), 0) == 0, bias, 0.0).astype(BF)
    wrows = 2 * width // len(table)
    devices = [(o ^ fo) * n_inner + (i ^ fi) for fo, fi in table]
    for k, out in enumerate((keep, give)):
        for j in range(len(table) // 2):
            rows = load_rows(wacc, devices[k * len(table) // 2 + j] * wrows, wrows)
            if wrows % 16 == 0:
                out[j * wrows : (j + 1) * wrows, :] = rows.astype(BF)
            else:
                wperm[j * wrows : (j + 1) * wrows, :] = rows
        if wrows % 16:
            out[0:width, :] = wperm[...].astype(BF)
        out[width : width + nhubs // 2, :] = hubf[k * nhubs // 2 : (k + 1) * nhubs // 2, :]
        out[width + nhubs // 2 :, :] = tail


def add_returned(acc, rows_ref, count_ref, blocks, returned):
    i = lax.axis_index("inner")
    tile = rows_ref.shape[1]
    for k in range(0, len(blocks), 2):
        some = blocks[k : k + 2]
        put = slot_onehot(rows_ref, count_ref, acc.shape[0], [i ^ d for d, _, _ in some])
        values = [returned[ref][at : at + tile, :] for _, ref, at in some]
        acc[...] += dot(put, values[0] if len(values) == 1 else jnp.concatenate(values, axis=0))


def first_scatter_kernel(blocks, count_ref, rows_ref, gown_ref, gp_ref, ws_ref, *rest):
    returned, out_ref = rest[:-1], rest[-1]
    out_ref[...] = gown_ref[...] + dot(gp_ref[...], ws_ref[...], NT)
    add_returned(out_ref, rows_ref, count_ref, blocks, returned)


def last_scatter_kernel(blocks, hub_ref, count_ref, rows_ref, own_ref, hub_grad_ref, *rest):
    returned, (out_ref, acc) = rest[:-2], rest[-2:]
    acc[...] = own_ref[...]
    add_returned(acc, rows_ref, count_ref, blocks, returned)
    for h in range(hub_ref.shape[0]):
        r = hub_ref[h]
        acc[pl.ds(r, 1), :] = acc[pl.ds(r, 1), :] + hub_grad_ref[h : h + 1, :]
    out_ref[...] = acc[...].astype(BF)


def finish_kernel(steps, n_inner, factor, x_ref, y_ref, bias_in, self_ref, neigh_ref, bias_ref, full):
    table = flips(steps)
    o = lax.axis_index("outer")
    i = lax.axis_index("inner")
    wrows = 2 * x_ref.shape[0] // len(table)
    width = self_ref.shape[0]
    for j, (fo, fi) in enumerate(table):
        d = (o ^ fo) * n_inner + (i ^ fi)
        ref, at = (x_ref, j) if 2 * j < len(table) else (y_ref, j - len(table) // 2)
        store_rows(full, d * wrows, ref[at * wrows : (at + 1) * wrows, :].astype(F32) * factor)
    self_ref[...] = full[0:width, :]
    neigh_ref[...] = full[width : 2 * width, :]
    bias_ref[...] = bias_in[0:1, :] * factor


def params(mib):
    return pltpu.CompilerParams(vmem_limit_bytes=mib * MIB)


def nbytes(scratch):
    return sum(s.dtype.itemsize * math.prod(s.shape) for s in scratch)


def cost(flops, nbytes):
    return pl.CostEstimate(flops=flops, bytes_accessed=nbytes, transcendentals=0)


def body(
    features,
    adj_tiles,
    tile_src,
    send_rows,
    send_count,
    hub_rows,
    w_self,
    w_neigh,
    out_bias,
    cotangent,
):
    n_outer, n_inner = lax.axis_size("outer"), lax.axis_size("inner")
    ndevice = n_outer * n_inner
    nrows, width = features.shape
    tile = adj_tiles.shape[1]
    nblocks, per_block = tile_src.shape
    hd = hub_rows.shape[0]
    nhubs = hd * ndevice
    ntiles = nblocks + n_inner + nhubs // tile
    groups = tree_groups(n_outer, n_inner)
    steps = sum(groups, [])
    hub_steps = sum(groups[::-1], [])
    wrows = 2 * width // ndevice

    def shape(*dims, dtype=BF):
        return jax.ShapeDtypeStruct(dims, dtype)

    blocks = sent_blocks(n_inner)
    sizes = tuple(shape(tile * len(some), width) for some in blocks)
    hub_own, own_rows, *outgoing, one, far_a, far_b = pl.pallas_call(
        gather_kernel,
        out_shape=(shape(hd, width),) + sizes,
        in_specs=[SM, SM, VM, VM],
        out_specs=(VM,) * (1 + len(sizes)),
        compiler_params=params(60),
        cost_estimate=cost(4 * 10**8, 3 * 10**6),
        name="gather_rows",
    )(hub_rows, send_count, features, send_rows)
    relays = relayed(n_inner)
    pairs = [exchange(p, (0, c)) for p, c in zip(outgoing, relays)]
    hubx = hub_own
    for group in groups[:-1]:
        hubx = spread(hubx, group)
    hubx, pairs, far_a, far_b = lax.optimization_barrier((hubx, pairs, far_a, far_b))
    direct = [exchange(far_a, (0, n_inner - 2)), exchange(far_b, (0, n_inner - 1))]
    hubx = spread(hubx, groups[-1])
    received = [own_rows, *pairs, relay(pairs, one), *direct]
    feat_t, adj_cat, adj_t, neigh_low, neigh_t, cot_wide = pl.pallas_call(
        prepare_kernel,
        out_shape=(
            shape(width, nrows),
            shape(nblocks, tile, per_block * tile),
            shape(nblocks, per_block * tile, tile),
            shape(width, width),
            shape(width, width),
            shape(nrows, width, dtype=F32),
        ),
        in_specs=[VM] * 4,
        out_specs=(VM,) * 6,
        compiler_params=params(8 + 4 * nbytes([adj_tiles]) // MIB),
        cost_estimate=cost(10**6, 7 * 10**6),
        name="prepare",
    )(features, adj_tiles, w_neigh, cotangent)
    self_low = w_self.astype(BF)
    pre0 = jnp.dot(features, self_low, preferred_element_type=F32) + out_bias

    half = width + nhubs // 2 + 16
    scratch = [
        pltpu.VMEM((ntiles, tile, width), BF),
        pltpu.VMEM((nrows, width), BF),
        pltpu.VMEM((ntiles, tile, width), F32),
        pltpu.VMEM((2 * width, width), F32),
        pltpu.VMEM((width, width) if wrows % 16 else (8, 128), F32),
        pltpu.VMEM((nhubs, width), BF),
    ]
    out_shape = (
        shape(nrows, width, dtype=F32),
        shape(nrows, width),
        shape(nrows, width, dtype=F32),
        shape(half, width),
        shape(half, width),
    ) + sizes
    operands = (
        features.reshape(nblocks, tile, width),
        feat_t,
        hubx,
        adj_cat,
        adj_t,
        pre0,
        neigh_low,
        neigh_t,
        cot_wide,
        *received,
    )
    pre, gp, gown, keep, give, *back = pl.pallas_call(
        functools.partial(middle_kernel, steps, hub_steps, n_inner),
        out_shape=out_shape,
        in_specs=[SM] + [VM] * len(operands),
        out_specs=(VM,) * len(out_shape),
        scratch_shapes=scratch,
        compiler_params=params(nbytes([*scratch, *operands, *out_shape]) // MIB + 8),
        cost_estimate=cost(2 * 10**9, 9 * 10**6),
        name="middle",
    )(tile_src, *operands)
    hidden_out = (pre * jax.nn.sigmoid(pre)).astype(BF)

    back_own, *back, back_one, back_a, back_b = back

    def reduce(parts, group):
        ways = 2 ** len(group)
        seg = [p.shape[0] // ways for p in parts[:2]]
        sends = []
        for c in range(1, ways):
            rows = [p[c * n : (c + 1) * n] for p, n in zip(parts, seg)]
            sends.append(jnp.concatenate(rows + [parts[2]], 0).astype(BF))
        w, hub, bias = parts[0][: seg[0]], parts[1][: seg[1]], parts[2]
        for flip, send in zip(flips(group)[1:], sends):
            got = exchange(send, flip).astype(F32)
            w, hub, bias = w + got[: seg[0]], hub + got[seg[0] : seg[0] + seg[1]], bias + got[seg[0] + seg[1] :]
        return w, hub, bias

    tie = lax.optimization_barrier
    pairs = [exchange(p, (0, c)) for p, c in zip(back, relays)]
    got = exchange(give, flips(groups[0])[1])
    part = keep.astype(F32) + got.astype(F32)
    parts = (part[:width], part[width : width + nhubs // 2], part[width + nhubs // 2 : width + nhubs // 2 + 8])
    for group in groups[1:-1]:
        parts = reduce(parts, group)
    parts, back_one = tie((parts, back_one))
    near = relay(pairs, back_one)
    part, hub_grad, bias_sum = reduce(parts, groups[-1])
    mine, hidden_out, back_a, back_b = tie((part.astype(BF), hidden_out, back_a, back_b))
    direct = [exchange(back_a, (0, n_inner - 2)), exchange(back_b, (0, n_inner - 1))]
    gathered = spread(mine, groups[-1])
    gathered, near = tie((gathered, near))
    for group in groups[1:-1][::-1]:
        gathered = spread(gathered, group)
    gathered, direct = tie((gathered, direct))

    where = places(n_inner, tile)
    first = [(d, k, at) for d, (k, at) in where.items() if d < n_inner - 2]
    own = pl.pallas_call(
        functools.partial(first_scatter_kernel, first),
        out_shape=shape(nrows, width, dtype=F32),
        in_specs=[SM] + [VM] * (6 + len(pairs)),
        out_specs=VM,
        compiler_params=params(16),
        cost_estimate=cost(4 * 10**8, 3 * 10**6),
        name="scatter_first",
    )(send_count, send_rows, gown, gp, self_low, back_own, *pairs, near)
    gathered, own = lax.optimization_barrier((gathered, own))
    other = exchange(gathered, flips(groups[0])[1])
    grad_features = pl.pallas_call(
        functools.partial(last_scatter_kernel, [(n_inner - 2, 0, 0), (n_inner - 1, 1, 0)]),
        out_shape=shape(nrows, width),
        in_specs=[SM, SM] + [VM] * 5,
        out_specs=VM,
        scratch_shapes=[pltpu.VMEM((nrows, width), F32)],
        compiler_params=params(16),
        cost_estimate=cost(2 * 10**8, 2 * 10**6),
        name="scatter_last",
    )(hub_rows, send_count, send_rows, own, hub_grad, *direct)
    factor = 1.0 / float(nrows * ndevice) ** 0.5
    total_self, total_neigh, total_bias = pl.pallas_call(
        functools.partial(finish_kernel, steps, n_inner, factor),
        out_shape=(shape(width, width, dtype=F32),) * 2 + (shape(1, width, dtype=F32),),
        in_specs=[VM] * 3,
        out_specs=(VM,) * 3,
        scratch_shapes=[pltpu.VMEM((2 * width, width), F32)],
        compiler_params=params(16),
        cost_estimate=cost(10**6, 3 * 10**6),
        name="finish",
    )(gathered, other, bias_sum)
    return hidden_out, grad_features, total_self, total_neigh, total_bias.reshape(width)


def solution(mesh):
    both = ("outer", "inner")
    return jax.shard_map(
        body,
        mesh=mesh,
        in_specs=(
            P(both, None),
            P(both, None, None),
            P(both, None),
            P(both, None),
            P(both, None),
            P(both),
            P(),
            P(),
            P(),
            P(both, None),
        ),
        out_specs=(P(both, None), P(both, None), P(), P(), P()),
        check_vma=False,
    )
```

```python
import functools
import math

import jax
import jax.numpy as jnp
from jax import lax
from jax.experimental import pallas as pl
from jax.experimental.pallas import tpu as pltpu
from jax.sharding import PartitionSpec as P

BF = jnp.bfloat16
F32 = jnp.float32
VM = pl.BlockSpec(memory_space=pltpu.VMEM)
SM = pl.BlockSpec(memory_space=pltpu.SMEM)
MIB = 1024 * 1024
TN = (((0,), (0,)), ((), ()))
NT = (((1,), (1,)), ((), ()))


def dot(a, b, dims=(((1,), (0,)), ((), ()))):
    return lax.dot_general(a, b, dims, preferred_element_type=F32)


def tree_groups(n_outer, n_inner):
    steps = []
    bit = 1
    while bit < n_outer:
        steps.append((bit, 0))
        bit *= 2
    bit = 1
    while bit < n_inner:
        steps.append((0, bit))
        bit *= 2
    middle = steps[1:-2]
    return [steps[:1]] + [middle[k : k + 2] for k in range(0, len(middle), 2)] + [steps[-2:]]


def flips(steps):
    count = len(steps)
    table = []
    for slot in range(2**count):
        fo = fi = 0
        for k, (bo, bi) in enumerate(steps):
            if (slot >> (count - 1 - k)) & 1:
                fo, fi = fo ^ bo, fi ^ bi
        table.append((fo, fi))
    return table


def hub_order(steps, n_inner, hd, nhubs):
    me = lax.axis_index("outer") * n_inner + lax.axis_index("inner")
    column = lax.broadcasted_iota(jnp.int32, (1, nhubs), 1)
    slot = column // hd
    flip = jnp.zeros((1, nhubs), jnp.int32)
    for k, (bo, bi) in enumerate(steps):
        flip = flip + ((slot >> (len(steps) - 1 - k)) & 1) * (bo * n_inner + bi)
    target = (flip ^ me) * hd + column % hd
    row = lax.broadcasted_iota(jnp.int32, (nhubs, nhubs), 0)
    return (row == target).astype(F32).astype(BF)


def load_rows(ref, at, n):
    if n % 8 == 0:
        return ref[pl.ds(pl.multiple_of(at, n), n), :]
    return jnp.concatenate([ref[pl.ds(at + r, 1), :] for r in range(n)], axis=0)


def store_rows(ref, at, value):
    n = value.shape[0]
    if n % 8 == 0:
        ref[pl.ds(pl.multiple_of(at, n), n), :] = value
    else:
        for r in range(n):
            ref[pl.ds(at + r, 1), :] = value[r : r + 1, :]


def exchange(x, flip):
    n_outer, n_inner = lax.axis_size("outer"), lax.axis_size("inner")
    mask = flip[0] * n_inner + flip[1]
    return lax.ppermute(x, ("outer", "inner"), [(s, s ^ mask) for s in range(n_outer * n_inner)])


def spread(x, group):
    parts = [x] + [exchange(x, flip) for flip in flips(group)[1:]]
    return lax.optimization_barrier(jnp.concatenate(parts, 0))


def relayed(n_inner):
    return list(range(2, n_inner - 2, 2))


def places(n_inner, tile):
    pairs = relayed(n_inner)
    near = 1 + len(pairs)
    where = {0: (0, 0), 1: (near, 0), n_inner - 2: (near + 1, 0), n_inner - 1: (near + 2, 0)}
    for k, c in enumerate(pairs):
        where[c] = (1 + k, 0)
        where[c + 1] = (near, (1 + k) * tile)
    return where


def sent_blocks(n_inner):
    return [[0]] + [[c, c + 1] for c in relayed(n_inner)] + [[1], [n_inner - 2], [n_inner - 1]]


def relay(pairs, one):
    rows = one.shape[0]
    return exchange(jnp.concatenate([one] + [p[rows:] for p in pairs], 0), (0, 1))


def slot_onehot(rows_ref, count_ref, nrows, partners):
    slots = rows_ref.shape[1]
    sub = lax.broadcasted_iota(jnp.int32, (nrows, slots), 0)
    lane = lax.broadcasted_iota(jnp.int32, (1, slots), 1)
    parts = []
    for q in partners:
        live = jnp.where(lane < count_ref[0, q], rows_ref[pl.ds(q, 1), :], -1)
        parts.append((sub == live).astype(F32).astype(BF))
    return jnp.concatenate(parts, axis=1)


def gather_kernel(hub_ref, count_ref, feat_ref, rows_ref, hub_out_ref, *outs):
    nrows = feat_ref.shape[0]
    n_inner, slots = rows_ref.shape
    nhub = hub_ref.shape[0]
    i = lax.axis_index("inner")
    feat = feat_ref[...]
    sub = lax.broadcasted_iota(jnp.int32, (16, nrows), 0)
    lane = lax.broadcasted_iota(jnp.int32, (16, nrows), 1)
    hot = jnp.zeros((16, nrows), F32)
    for h in range(nhub):
        hot = hot + ((sub == h) & (lane == hub_ref[h])).astype(F32)
    hub_out_ref[...] = dot(hot.astype(BF), feat)[:nhub].astype(BF)
    blocks = sent_blocks(n_inner)
    order = [d for some in blocks for d in some]
    pick = slot_onehot(rows_ref, count_ref, nrows, [i ^ d for d in order])
    rows = dot(pick, feat, TN).astype(BF)
    at = 0
    for some, out in zip(blocks, outs):
        out[...] = rows[at * slots : (at + len(some)) * slots, :]
        at += len(some)


def prepare_kernel(feat_ref, adj_ref, wn_ref, cot_ref, feat_t, adj_cat, adj_t, wn_low, wn_t, cot_wide):
    feat_t[...] = feat_ref[...].T
    nblocks, tile, _ = adj_cat.shape
    per_block = adj_ref.shape[0] // nblocks
    for b in range(nblocks):
        for t in range(per_block):
            block = adj_ref[b * per_block + t]
            adj_cat[b, :, t * tile : (t + 1) * tile] = block
            adj_t[b, t * tile : (t + 1) * tile, :] = block.T
    low = wn_ref[...].astype(BF)
    wn_low[...] = low
    wn_t[...] = low.T
    cot_wide[...] = cot_ref[...].astype(F32)


def middle_kernel(
    steps,
    hub_steps,
    n_inner,
    tile_src,
    feat,
    feat_t,
    hubx,
    adj_cat,
    adj_t,
    pre0,
    wn,
    wn_t,
    cot,
    *rest,
):
    count = (len(rest) - 11) // 2
    recv, (pre_out, gp_out, gown, keep, give), rest = rest[:count], rest[count : count + 5], rest[count + 5 :]
    back, (src, agg, gsrc, wacc, wperm, hubf) = rest[:count], rest[count:]
    o = lax.axis_index("outer")
    i = lax.axis_index("inner")
    table = flips(steps)
    nblocks, per_block = tile_src.shape
    tile = adj_cat.shape[1]
    nrows, width = cot.shape
    ntiles = src.shape[0]
    first_hub = nblocks + n_inner
    nhubs = hubx.shape[0]
    hd = nhubs // len(table)
    src[0:nblocks] = feat[...]
    for d, (k, at) in places(n_inner, tile).items():
        src[nblocks + (i ^ d)] = recv[k][at : at + tile, :]
    order = hub_order(hub_steps, n_inner, hd, nhubs)
    src[first_hub:] = dot(order, hubx[...]).astype(BF).reshape(ntiles - first_hub, tile, width)
    for b in range(nblocks):
        acc = jnp.zeros((tile, width), F32)
        for t in range(0, per_block, 2):
            ts = range(t, min(t + 2, per_block))
            rhs = [src[tile_src[b, u]] for u in ts]
            rhs = rhs[0] if len(rhs) == 1 else jnp.concatenate(rhs, axis=0)
            acc = acc + dot(adj_cat[b, :, t * tile : (t + len(ts)) * tile], rhs)
        agg[b * tile : (b + 1) * tile, :] = acc.astype(BF)
    pre = pre0[...] + dot(agg[...], wn[...])
    pre_out[...] = pre
    sig = jax.nn.sigmoid(pre)
    gp = (cot[...] * sig * (1.0 + pre * (1.0 - sig))).astype(BF)
    gp_out[...] = gp
    gagg = dot(gp, wn_t[...]).astype(BF)
    gsrc[...] = jnp.zeros(gsrc.shape, F32)
    for b in range(nblocks):
        for t in range(0, per_block, 3):
            last = min(t + 3, per_block)
            some = dot(adj_t[b, t * tile : last * tile, :], gagg[b * tile : (b + 1) * tile, :])
            for u in range(t, last):
                s = tile_src[b, u]
                gsrc[s] = gsrc[s] + some[(u - t) * tile : (u - t + 1) * tile, :]
    for some, out in zip(sent_blocks(n_inner), back):
        for k, d in enumerate(some):
            out[k * tile : (k + 1) * tile, :] = gsrc[nblocks + (i ^ d)].astype(BF)
    gown[...] = gsrc[0:nblocks].reshape(nrows, width)
    wacc[0:width, :] = dot(feat_t[...], gp)
    wacc[width : 2 * width, :] = dot(agg[...], gp, TN)
    order = hub_order(steps, n_inner, hd, nhubs)
    hubf[...] = dot(order, gsrc[first_hub:].reshape(nhubs, width).astype(BF), TN).astype(BF)
    bias = jnp.sum(gp.astype(F32), axis=0, keepdims=True)
    tail = jnp.where(lax.broadcasted_iota(jnp.int32, (16, width), 0) == 0, bias, 0.0).astype(BF)
    wrows = 2 * width // len(table)
    devices = [(o ^ fo) * n_inner + (i ^ fi) for fo, fi in table]
    for k, out in enumerate((keep, give)):
        for j in range(len(table) // 2):
            rows = load_rows(wacc, devices[k * len(table) // 2 + j] * wrows, wrows)
            if wrows % 16 == 0:
                out[j * wrows : (j + 1) * wrows, :] = rows.astype(BF)
            else:
                wperm[j * wrows : (j + 1) * wrows, :] = rows
        if wrows % 16:
            out[0:width, :] = wperm[...].astype(BF)
        out[width : width + nhubs // 2, :] = hubf[k * nhubs // 2 : (k + 1) * nhubs // 2, :]
        out[width + nhubs // 2 :, :] = tail


def add_returned(acc, rows_ref, count_ref, blocks, returned):
    i = lax.axis_index("inner")
    tile = rows_ref.shape[1]
    for k in range(0, len(blocks), 2):
        some = blocks[k : k + 2]
        put = slot_onehot(rows_ref, count_ref, acc.shape[0], [i ^ d for d, _, _ in some])
        values = [returned[ref][at : at + tile, :] for _, ref, at in some]
        acc[...] += dot(put, values[0] if len(values) == 1 else jnp.concatenate(values, axis=0))


def first_scatter_kernel(blocks, count_ref, rows_ref, gown_ref, gp_ref, ws_ref, *rest):
    returned, out_ref = rest[:-1], rest[-1]
    out_ref[...] = gown_ref[...] + dot(gp_ref[...], ws_ref[...], NT)
    add_returned(out_ref, rows_ref, count_ref, blocks, returned)


def last_scatter_kernel(blocks, hub_ref, count_ref, rows_ref, own_ref, hub_grad_ref, *rest):
    returned, (out_ref, acc) = rest[:-2], rest[-2:]
    acc[...] = own_ref[...]
    add_returned(acc, rows_ref, count_ref, blocks, returned)
    for h in range(hub_ref.shape[0]):
        r = hub_ref[h]
        acc[pl.ds(r, 1), :] = acc[pl.ds(r, 1), :] + hub_grad_ref[h : h + 1, :]
    out_ref[...] = acc[...].astype(BF)


def finish_kernel(steps, n_inner, factor, x_ref, y_ref, bias_in, self_ref, neigh_ref, bias_ref, full):
    table = flips(steps)
    o = lax.axis_index("outer")
    i = lax.axis_index("inner")
    wrows = 2 * x_ref.shape[0] // len(table)
    width = self_ref.shape[0]
    for j, (fo, fi) in enumerate(table):
        d = (o ^ fo) * n_inner + (i ^ fi)
        ref, at = (x_ref, j) if 2 * j < len(table) else (y_ref, j - len(table) // 2)
        store_rows(full, d * wrows, ref[at * wrows : (at + 1) * wrows, :].astype(F32) * factor)
    self_ref[...] = full[0:width, :]
    neigh_ref[...] = full[width : 2 * width, :]
    bias_ref[...] = bias_in[0:1, :] * factor


def params(mib):
    return pltpu.CompilerParams(vmem_limit_bytes=mib * MIB)


def nbytes(scratch):
    return sum(s.dtype.itemsize * math.prod(s.shape) for s in scratch)


def cost(flops, nbytes):
    return pl.CostEstimate(flops=flops, bytes_accessed=nbytes, transcendentals=0)


def body(
    features,
    adj_tiles,
    tile_src,
    send_rows,
    send_count,
    hub_rows,
    w_self,
    w_neigh,
    out_bias,
    cotangent,
):
    n_outer, n_inner = lax.axis_size("outer"), lax.axis_size("inner")
    ndevice = n_outer * n_inner
    nrows, width = features.shape
    tile = adj_tiles.shape[1]
    nblocks, per_block = tile_src.shape
    hd = hub_rows.shape[0]
    nhubs = hd * ndevice
    ntiles = nblocks + n_inner + nhubs // tile
    groups = tree_groups(n_outer, n_inner)
    steps = sum(groups, [])
    hub_groups = groups[:-1] + [[step] for step in groups[-1]]
    hub_steps = sum(hub_groups[::-1], [])
    wrows = 2 * width // ndevice

    def shape(*dims, dtype=BF):
        return jax.ShapeDtypeStruct(dims, dtype)

    blocks = sent_blocks(n_inner)
    sizes = tuple(shape(tile * len(some), width) for some in blocks)
    hub_own, own_rows, *outgoing, one, far_a, far_b = pl.pallas_call(
        gather_kernel,
        out_shape=(shape(hd, width),) + sizes,
        in_specs=[SM, SM, VM, VM],
        out_specs=(VM,) * (1 + len(sizes)),
        compiler_params=params(60),
        cost_estimate=cost(4 * 10**8, 3 * 10**6),
        name="gather_rows",
    )(hub_rows, send_count, features, send_rows)
    relays = relayed(n_inner)
    pairs = [exchange(p, (0, c)) for p, c in zip(outgoing, relays)]
    hubx = hub_own
    for group in groups[:-1]:
        hubx = spread(hubx, group)
    hubx, pairs[0], far_a, far_b = lax.optimization_barrier((hubx, pairs[0], far_a, far_b))
    direct = [exchange(far_a, (0, n_inner - 2)), exchange(far_b, (0, n_inner - 1))]
    for group in hub_groups[-2:]:
        hubx = spread(hubx, group)
    received = [own_rows, *pairs, relay(pairs, one), *direct]
    feat_t, adj_cat, adj_t, neigh_low, neigh_t, cot_wide = pl.pallas_call(
        prepare_kernel,
        out_shape=(
            shape(width, nrows),
            shape(nblocks, tile, per_block * tile),
            shape(nblocks, per_block * tile, tile),
            shape(width, width),
            shape(width, width),
            shape(nrows, width, dtype=F32),
        ),
        in_specs=[VM] * 4,
        out_specs=(VM,) * 6,
        compiler_params=params(8 + 4 * nbytes([adj_tiles]) // MIB),
        cost_estimate=cost(10**6, 7 * 10**6),
        name="prepare",
    )(features, adj_tiles, w_neigh, cotangent)
    self_low = w_self.astype(BF)
    pre0 = jnp.dot(features, self_low, preferred_element_type=F32) + out_bias

    half = width + nhubs // 2 + 16
    scratch = [
        pltpu.VMEM((ntiles, tile, width), BF),
        pltpu.VMEM((nrows, width), BF),
        pltpu.VMEM((ntiles, tile, width), F32),
        pltpu.VMEM((2 * width, width), F32),
        pltpu.VMEM((width, width) if wrows % 16 else (8, 128), F32),
        pltpu.VMEM((nhubs, width), BF),
    ]
    out_shape = (
        shape(nrows, width, dtype=F32),
        shape(nrows, width),
        shape(nrows, width, dtype=F32),
        shape(half, width),
        shape(half, width),
    ) + sizes
    operands = (
        features.reshape(nblocks, tile, width),
        feat_t,
        hubx,
        adj_cat,
        adj_t,
        pre0,
        neigh_low,
        neigh_t,
        cot_wide,
        *received,
    )
    pre, gp, gown, keep, give, *back = pl.pallas_call(
        functools.partial(middle_kernel, steps, hub_steps, n_inner),
        out_shape=out_shape,
        in_specs=[SM] + [VM] * len(operands),
        out_specs=(VM,) * len(out_shape),
        scratch_shapes=scratch,
        compiler_params=params(nbytes([*scratch, *operands, *out_shape]) // MIB + 8),
        cost_estimate=cost(2 * 10**9, 9 * 10**6),
        name="middle",
    )(tile_src, *operands)
    hidden_out = (pre * jax.nn.sigmoid(pre)).astype(BF)

    back_own, *back, back_one, back_a, back_b = back

    def reduce(parts, group):
        ways = 2 ** len(group)
        seg = [p.shape[0] // ways for p in parts[:2]]
        sends = []
        for c in range(1, ways):
            rows = [p[c * n : (c + 1) * n] for p, n in zip(parts, seg)]
            sends.append(jnp.concatenate(rows + [parts[2]], 0).astype(BF))
        w, hub, bias = parts[0][: seg[0]], parts[1][: seg[1]], parts[2]
        for flip, send in zip(flips(group)[1:], sends):
            got = exchange(send, flip).astype(F32)
            w, hub, bias = w + got[: seg[0]], hub + got[seg[0] : seg[0] + seg[1]], bias + got[seg[0] + seg[1] :]
        return w, hub, bias

    tie = lax.optimization_barrier
    pairs = [exchange(p, (0, c)) for p, c in zip(back, relays)]
    got = exchange(give, flips(groups[0])[1])
    part = keep.astype(F32) + got.astype(F32)
    parts = (part[:width], part[width : width + nhubs // 2], part[width + nhubs // 2 : width + nhubs // 2 + 8])
    for group in groups[1:-1]:
        parts = reduce(parts, group)
    parts, back_one = tie((parts, back_one))
    near = relay(pairs, back_one)
    part, hub_grad, bias_sum = reduce(parts, groups[-1])
    mine, hidden_out, back_a, back_b = tie((part.astype(BF), hidden_out, back_a, back_b))
    direct = [exchange(back_a, (0, n_inner - 2)), exchange(back_b, (0, n_inner - 1))]
    gathered = spread(mine, groups[-1])
    gathered, near = tie((gathered, near))
    for group in groups[1:-1][::-1]:
        gathered = spread(gathered, group)
    gathered, direct = tie((gathered, direct))

    where = places(n_inner, tile)
    first = [(d, k, at) for d, (k, at) in where.items() if d < n_inner - 2]
    own = pl.pallas_call(
        functools.partial(first_scatter_kernel, first),
        out_shape=shape(nrows, width, dtype=F32),
        in_specs=[SM] + [VM] * (6 + len(pairs)),
        out_specs=VM,
        compiler_params=params(16),
        cost_estimate=cost(4 * 10**8, 3 * 10**6),
        name="scatter_first",
    )(send_count, send_rows, gown, gp, self_low, back_own, *pairs, near)
    gathered, own = lax.optimization_barrier((gathered, own))
    other = exchange(gathered, flips(groups[0])[1])
    grad_features = pl.pallas_call(
        functools.partial(last_scatter_kernel, [(n_inner - 2, 0, 0), (n_inner - 1, 1, 0)]),
        out_shape=shape(nrows, width),
        in_specs=[SM, SM] + [VM] * 5,
        out_specs=VM,
        scratch_shapes=[pltpu.VMEM((nrows, width), F32)],
        compiler_params=params(16),
        cost_estimate=cost(2 * 10**8, 2 * 10**6),
        name="scatter_last",
    )(hub_rows, send_count, send_rows, own, hub_grad, *direct)
    factor = 1.0 / float(nrows * ndevice) ** 0.5
    total_self, total_neigh, total_bias = pl.pallas_call(
        functools.partial(finish_kernel, steps, n_inner, factor),
        out_shape=(shape(width, width, dtype=F32),) * 2 + (shape(1, width, dtype=F32),),
        in_specs=[VM] * 3,
        out_specs=(VM,) * 3,
        scratch_shapes=[pltpu.VMEM((2 * width, width), F32)],
        compiler_params=params(16),
        cost_estimate=cost(10**6, 3 * 10**6),
        name="finish",
    )(gathered, other, bias_sum)
    return hidden_out, grad_features, total_self, total_neigh, total_bias.reshape(width)


def solution(mesh):
    both = ("outer", "inner")
    return jax.shard_map(
        body,
        mesh=mesh,
        in_specs=(
            P(both, None),
            P(both, None, None),
            P(both, None),
            P(both, None),
            P(both, None),
            P(both),
            P(),
            P(),
            P(),
            P(both, None),
        ),
        out_specs=(P(both, None), P(both, None), P(), P(), P()),
        check_vma=False,
    )
```

```python
import functools
import math

import jax
import jax.numpy as jnp
from jax import lax
from jax.experimental import pallas as pl
from jax.experimental.pallas import tpu as pltpu
from jax.sharding import PartitionSpec as P

BF = jnp.bfloat16
F32 = jnp.float32
VM = pl.BlockSpec(memory_space=pltpu.VMEM)
SM = pl.BlockSpec(memory_space=pltpu.SMEM)
MIB = 1024 * 1024
TN = (((0,), (0,)), ((), ()))
NT = (((1,), (1,)), ((), ()))


def dot(a, b, dims=(((1,), (0,)), ((), ()))):
    return lax.dot_general(a, b, dims, preferred_element_type=F32)


def tree_groups(n_outer, n_inner):
    steps = []
    bit = 1
    while bit < n_outer:
        steps.append((bit, 0))
        bit *= 2
    bit = 1
    while bit < n_inner:
        steps.append((0, bit))
        bit *= 2
    middle = steps[1:-2]
    return [steps[:1]] + [middle[k : k + 2] for k in range(0, len(middle), 2)] + [steps[-2:]]


def flips(steps):
    count = len(steps)
    table = []
    for slot in range(2**count):
        fo = fi = 0
        for k, (bo, bi) in enumerate(steps):
            if (slot >> (count - 1 - k)) & 1:
                fo, fi = fo ^ bo, fi ^ bi
        table.append((fo, fi))
    return table


def hub_order(steps, n_inner, hd, nhubs):
    me = lax.axis_index("outer") * n_inner + lax.axis_index("inner")
    column = lax.broadcasted_iota(jnp.int32, (1, nhubs), 1)
    slot = column // hd
    flip = jnp.zeros((1, nhubs), jnp.int32)
    for k, (bo, bi) in enumerate(steps):
        flip = flip + ((slot >> (len(steps) - 1 - k)) & 1) * (bo * n_inner + bi)
    target = (flip ^ me) * hd + column % hd
    row = lax.broadcasted_iota(jnp.int32, (nhubs, nhubs), 0)
    return (row == target).astype(F32).astype(BF)


def load_rows(ref, at, n):
    if n % 8 == 0:
        return ref[pl.ds(pl.multiple_of(at, n), n), :]
    return jnp.concatenate([ref[pl.ds(at + r, 1), :] for r in range(n)], axis=0)


def store_rows(ref, at, value):
    n = value.shape[0]
    if n % 8 == 0:
        ref[pl.ds(pl.multiple_of(at, n), n), :] = value
    else:
        for r in range(n):
            ref[pl.ds(at + r, 1), :] = value[r : r + 1, :]


def exchange(x, flip):
    n_outer, n_inner = lax.axis_size("outer"), lax.axis_size("inner")
    mask = flip[0] * n_inner + flip[1]
    return lax.ppermute(x, ("outer", "inner"), [(s, s ^ mask) for s in range(n_outer * n_inner)])


def spread(x, group):
    parts = [x] + [exchange(x, flip) for flip in flips(group)[1:]]
    return lax.optimization_barrier(jnp.concatenate(parts, 0))


def relayed(n_inner):
    return list(range(n_inner - 4, 0, -2))


def places(n_inner, tile):
    pairs = relayed(n_inner)
    near = 1 + len(pairs)
    where = {0: (0, 0), 1: (near, 0), n_inner - 2: (near + 1, 0), n_inner - 1: (near + 2, 0)}
    for k, c in enumerate(pairs):
        where[c] = (1 + k, 0)
        where[c + 1] = (near, (1 + k) * tile)
    return where


def sent_blocks(n_inner):
    return [[0]] + [[c, c + 1] for c in relayed(n_inner)] + [[1], [n_inner - 2], [n_inner - 1]]


def relay(pairs, one):
    rows = one.shape[0]
    return exchange(jnp.concatenate([one] + [p[rows:] for p in pairs], 0), (0, 1))


def slot_onehot(rows_ref, count_ref, nrows, partners):
    slots = rows_ref.shape[1]
    sub = lax.broadcasted_iota(jnp.int32, (nrows, slots), 0)
    lane = lax.broadcasted_iota(jnp.int32, (1, slots), 1)
    parts = []
    for q in partners:
        live = jnp.where(lane < count_ref[0, q], rows_ref[pl.ds(q, 1), :], -1)
        parts.append((sub == live).astype(F32).astype(BF))
    return jnp.concatenate(parts, axis=1)


def gather_kernel(hub_ref, count_ref, feat_ref, rows_ref, hub_out_ref, *outs):
    nrows = feat_ref.shape[0]
    n_inner, slots = rows_ref.shape
    nhub = hub_ref.shape[0]
    i = lax.axis_index("inner")
    feat = feat_ref[...]
    sub = lax.broadcasted_iota(jnp.int32, (16, nrows), 0)
    lane = lax.broadcasted_iota(jnp.int32, (16, nrows), 1)
    hot = jnp.zeros((16, nrows), F32)
    for h in range(nhub):
        hot = hot + ((sub == h) & (lane == hub_ref[h])).astype(F32)
    hub_out_ref[...] = dot(hot.astype(BF), feat)[:nhub].astype(BF)
    blocks = sent_blocks(n_inner)
    order = [d for some in blocks for d in some]
    pick = slot_onehot(rows_ref, count_ref, nrows, [i ^ d for d in order])
    rows = dot(pick, feat, TN).astype(BF)
    at = 0
    for some, out in zip(blocks, outs):
        out[...] = rows[at * slots : (at + len(some)) * slots, :]
        at += len(some)


def prepare_kernel(feat_ref, adj_ref, wn_ref, cot_ref, feat_t, adj_cat, adj_t, wn_low, wn_t, cot_wide):
    feat_t[...] = feat_ref[...].T
    nblocks, tile, _ = adj_cat.shape
    per_block = adj_ref.shape[0] // nblocks
    for b in range(nblocks):
        for t in range(per_block):
            block = adj_ref[b * per_block + t]
            adj_cat[b, :, t * tile : (t + 1) * tile] = block
            adj_t[b, t * tile : (t + 1) * tile, :] = block.T
    low = wn_ref[...].astype(BF)
    wn_low[...] = low
    wn_t[...] = low.T
    cot_wide[...] = cot_ref[...].astype(F32)


def middle_kernel(
    steps,
    hub_steps,
    n_inner,
    tile_src,
    feat,
    feat_t,
    hubx,
    adj_cat,
    adj_t,
    pre0,
    wn,
    wn_t,
    cot,
    *rest,
):
    count = (len(rest) - 11) // 2
    recv, (pre_out, gp_out, gown, keep, give), rest = rest[:count], rest[count : count + 5], rest[count + 5 :]
    back, (src, agg, gsrc, wacc, wperm, hubf) = rest[:count], rest[count:]
    o = lax.axis_index("outer")
    i = lax.axis_index("inner")
    table = flips(steps)
    nblocks, per_block = tile_src.shape
    tile = adj_cat.shape[1]
    nrows, width = cot.shape
    ntiles = src.shape[0]
    first_hub = nblocks + n_inner
    nhubs = hubx.shape[0]
    hd = nhubs // len(table)
    src[0:nblocks] = feat[...]
    for d, (k, at) in places(n_inner, tile).items():
        src[nblocks + (i ^ d)] = recv[k][at : at + tile, :]
    order = hub_order(hub_steps, n_inner, hd, nhubs)
    src[first_hub:] = dot(order, hubx[...]).astype(BF).reshape(ntiles - first_hub, tile, width)
    for b in range(nblocks):
        acc = jnp.zeros((tile, width), F32)
        for t in range(0, per_block, 2):
            ts = range(t, min(t + 2, per_block))
            rhs = [src[tile_src[b, u]] for u in ts]
            rhs = rhs[0] if len(rhs) == 1 else jnp.concatenate(rhs, axis=0)
            acc = acc + dot(adj_cat[b, :, t * tile : (t + len(ts)) * tile], rhs)
        agg[b * tile : (b + 1) * tile, :] = acc.astype(BF)
    pre = pre0[...] + dot(agg[...], wn[...])
    pre_out[...] = pre
    sig = jax.nn.sigmoid(pre)
    gp = (cot[...] * sig * (1.0 + pre * (1.0 - sig))).astype(BF)
    gp_out[...] = gp
    gagg = dot(gp, wn_t[...]).astype(BF)
    gsrc[...] = jnp.zeros(gsrc.shape, F32)
    for b in range(nblocks):
        for t in range(0, per_block, 3):
            last = min(t + 3, per_block)
            some = dot(adj_t[b, t * tile : last * tile, :], gagg[b * tile : (b + 1) * tile, :])
            for u in range(t, last):
                s = tile_src[b, u]
                gsrc[s] = gsrc[s] + some[(u - t) * tile : (u - t + 1) * tile, :]
    for some, out in zip(sent_blocks(n_inner), back):
        for k, d in enumerate(some):
            out[k * tile : (k + 1) * tile, :] = gsrc[nblocks + (i ^ d)].astype(BF)
    gown[...] = gsrc[0:nblocks].reshape(nrows, width)
    wacc[0:width, :] = dot(feat_t[...], gp)
    wacc[width : 2 * width, :] = dot(agg[...], gp, TN)
    order = hub_order(steps, n_inner, hd, nhubs)
    hubf[...] = dot(order, gsrc[first_hub:].reshape(nhubs, width).astype(BF), TN).astype(BF)
    bias = jnp.sum(gp.astype(F32), axis=0, keepdims=True)
    tail = jnp.where(lax.broadcasted_iota(jnp.int32, (16, width), 0) == 0, bias, 0.0).astype(BF)
    wrows = 2 * width // len(table)
    devices = [(o ^ fo) * n_inner + (i ^ fi) for fo, fi in table]
    for k, out in enumerate((keep, give)):
        for j in range(len(table) // 2):
            rows = load_rows(wacc, devices[k * len(table) // 2 + j] * wrows, wrows)
            if wrows % 16 == 0:
                out[j * wrows : (j + 1) * wrows, :] = rows.astype(BF)
            else:
                wperm[j * wrows : (j + 1) * wrows, :] = rows
        if wrows % 16:
            out[0:width, :] = wperm[...].astype(BF)
        out[width : width + nhubs // 2, :] = hubf[k * nhubs // 2 : (k + 1) * nhubs // 2, :]
        out[width + nhubs // 2 :, :] = tail


def add_returned(acc, rows_ref, count_ref, blocks, returned):
    i = lax.axis_index("inner")
    tile = rows_ref.shape[1]
    for k in range(0, len(blocks), 2):
        some = blocks[k : k + 2]
        put = slot_onehot(rows_ref, count_ref, acc.shape[0], [i ^ d for d, _, _ in some])
        values = [returned[ref][at : at + tile, :] for _, ref, at in some]
        acc[...] += dot(put, values[0] if len(values) == 1 else jnp.concatenate(values, axis=0))


def first_scatter_kernel(blocks, count_ref, rows_ref, gown_ref, gp_ref, ws_ref, *rest):
    returned, out_ref = rest[:-1], rest[-1]
    out_ref[...] = gown_ref[...] + dot(gp_ref[...], ws_ref[...], NT)
    add_returned(out_ref, rows_ref, count_ref, blocks, returned)


def last_scatter_kernel(blocks, hub_ref, count_ref, rows_ref, own_ref, hub_grad_ref, *rest):
    returned, (out_ref, acc) = rest[:-2], rest[-2:]
    acc[...] = own_ref[...]
    add_returned(acc, rows_ref, count_ref, blocks, returned)
    for h in range(hub_ref.shape[0]):
        r = hub_ref[h]
        acc[pl.ds(r, 1), :] = acc[pl.ds(r, 1), :] + hub_grad_ref[h : h + 1, :]
    out_ref[...] = acc[...].astype(BF)


def finish_kernel(steps, n_inner, factor, x_ref, y_ref, bias_in, self_ref, neigh_ref, bias_ref, full):
    table = flips(steps)
    o = lax.axis_index("outer")
    i = lax.axis_index("inner")
    wrows = 2 * x_ref.shape[0] // len(table)
    width = self_ref.shape[0]
    for j, (fo, fi) in enumerate(table):
        d = (o ^ fo) * n_inner + (i ^ fi)
        ref, at = (x_ref, j) if 2 * j < len(table) else (y_ref, j - len(table) // 2)
        store_rows(full, d * wrows, ref[at * wrows : (at + 1) * wrows, :].astype(F32) * factor)
    self_ref[...] = full[0:width, :]
    neigh_ref[...] = full[width : 2 * width, :]
    bias_ref[...] = bias_in[0:1, :] * factor


def params(mib):
    return pltpu.CompilerParams(vmem_limit_bytes=mib * MIB)


def nbytes(scratch):
    return sum(s.dtype.itemsize * math.prod(s.shape) for s in scratch)


def cost(flops, nbytes):
    return pl.CostEstimate(flops=flops, bytes_accessed=nbytes, transcendentals=0)


def body(
    features,
    adj_tiles,
    tile_src,
    send_rows,
    send_count,
    hub_rows,
    w_self,
    w_neigh,
    out_bias,
    cotangent,
):
    n_outer, n_inner = lax.axis_size("outer"), lax.axis_size("inner")
    ndevice = n_outer * n_inner
    nrows, width = features.shape
    tile = adj_tiles.shape[1]
    nblocks, per_block = tile_src.shape
    hd = hub_rows.shape[0]
    nhubs = hd * ndevice
    ntiles = nblocks + n_inner + nhubs // tile
    groups = tree_groups(n_outer, n_inner)
    steps = sum(groups, [])
    hub_groups = groups[:-1] + [[step] for step in groups[-1]]
    hub_steps = sum(hub_groups[::-1], [])
    wrows = 2 * width // ndevice

    def shape(*dims, dtype=BF):
        return jax.ShapeDtypeStruct(dims, dtype)

    blocks = sent_blocks(n_inner)
    sizes = tuple(shape(tile * len(some), width) for some in blocks)
    hub_own, own_rows, *outgoing, one, far_a, far_b = pl.pallas_call(
        gather_kernel,
        out_shape=(shape(hd, width),) + sizes,
        in_specs=[SM, SM, VM, VM],
        out_specs=(VM,) * (1 + len(sizes)),
        compiler_params=params(60),
        cost_estimate=cost(4 * 10**8, 3 * 10**6),
        name="gather_rows",
    )(hub_rows, send_count, features, send_rows)
    relays = relayed(n_inner)
    pairs = [exchange(p, (0, c)) for p, c in zip(outgoing, relays)]
    hubx = hub_own
    for group in groups[:-1]:
        hubx = spread(hubx, group)
    pairs[-1], far_a, far_b = lax.optimization_barrier((pairs[-1], far_a, far_b))
    direct = [exchange(far_a, (0, n_inner - 2)), exchange(far_b, (0, n_inner - 1))]
    for group in hub_groups[-2:]:
        hubx = spread(hubx, group)
    received = [own_rows, *pairs, relay(pairs, one), *direct]
    feat_t, adj_cat, adj_t, neigh_low, neigh_t, cot_wide = pl.pallas_call(
        prepare_kernel,
        out_shape=(
            shape(width, nrows),
            shape(nblocks, tile, per_block * tile),
            shape(nblocks, per_block * tile, tile),
            shape(width, width),
            shape(width, width),
            shape(nrows, width, dtype=F32),
        ),
        in_specs=[VM] * 4,
        out_specs=(VM,) * 6,
        compiler_params=params(8 + 4 * nbytes([adj_tiles]) // MIB),
        cost_estimate=cost(10**6, 7 * 10**6),
        name="prepare",
    )(features, adj_tiles, w_neigh, cotangent)
    self_low = w_self.astype(BF)
    pre0 = jnp.dot(features, self_low, preferred_element_type=F32) + out_bias

    half = width + nhubs // 2 + 16
    scratch = [
        pltpu.VMEM((ntiles, tile, width), BF),
        pltpu.VMEM((nrows, width), BF),
        pltpu.VMEM((ntiles, tile, width), F32),
        pltpu.VMEM((2 * width, width), F32),
        pltpu.VMEM((width, width) if wrows % 16 else (8, 128), F32),
        pltpu.VMEM((nhubs, width), BF),
    ]
    out_shape = (
        shape(nrows, width, dtype=F32),
        shape(nrows, width),
        shape(nrows, width, dtype=F32),
        shape(half, width),
        shape(half, width),
    ) + sizes
    operands = (
        features.reshape(nblocks, tile, width),
        feat_t,
        hubx,
        adj_cat,
        adj_t,
        pre0,
        neigh_low,
        neigh_t,
        cot_wide,
        *received,
    )
    pre, gp, gown, keep, give, *back = pl.pallas_call(
        functools.partial(middle_kernel, steps, hub_steps, n_inner),
        out_shape=out_shape,
        in_specs=[SM] + [VM] * len(operands),
        out_specs=(VM,) * len(out_shape),
        scratch_shapes=scratch,
        compiler_params=params(nbytes([*scratch, *operands, *out_shape]) // MIB + 8),
        cost_estimate=cost(2 * 10**9, 9 * 10**6),
        name="middle",
    )(tile_src, *operands)
    hidden_out = (pre * jax.nn.sigmoid(pre)).astype(BF)

    back_own, *back, back_one, back_a, back_b = back

    def reduce(parts, group):
        ways = 2 ** len(group)
        seg = [p.shape[0] // ways for p in parts[:2]]
        sends = []
        for c in range(1, ways):
            rows = [p[c * n : (c + 1) * n] for p, n in zip(parts, seg)]
            sends.append(jnp.concatenate(rows + [parts[2]], 0).astype(BF))
        w, hub, bias = parts[0][: seg[0]], parts[1][: seg[1]], parts[2]
        for flip, send in zip(flips(group)[1:], sends):
            got = exchange(send, flip).astype(F32)
            w, hub, bias = w + got[: seg[0]], hub + got[seg[0] : seg[0] + seg[1]], bias + got[seg[0] + seg[1] :]
        return w, hub, bias

    tie = lax.optimization_barrier
    pairs = [exchange(p, (0, c)) for p, c in zip(back, relays)]
    got = exchange(give, flips(groups[0])[1])
    part = keep.astype(F32) + got.astype(F32)
    parts = (part[:width], part[width : width + nhubs // 2], part[width + nhubs // 2 : width + nhubs // 2 + 8])
    for group in groups[1:-1]:
        parts = reduce(parts, group)
    parts, back_one = tie((parts, back_one))
    near = relay(pairs, back_one)
    part, hub_grad, bias_sum = reduce(parts, groups[-1])
    mine, hidden_out, back_a, back_b = tie((part.astype(BF), hidden_out, back_a, back_b))
    direct = [exchange(back_a, (0, n_inner - 2)), exchange(back_b, (0, n_inner - 1))]
    gathered = spread(mine, groups[-1])
    gathered, near = tie((gathered, near))
    for group in groups[1:-1][::-1]:
        gathered = spread(gathered, group)
    gathered, direct = tie((gathered, direct))

    where = places(n_inner, tile)
    first = [(d, k, at) for d, (k, at) in where.items() if d < n_inner - 2]
    own = pl.pallas_call(
        functools.partial(first_scatter_kernel, first),
        out_shape=shape(nrows, width, dtype=F32),
        in_specs=[SM] + [VM] * (6 + len(pairs)),
        out_specs=VM,
        compiler_params=params(16),
        cost_estimate=cost(4 * 10**8, 3 * 10**6),
        name="scatter_first",
    )(send_count, send_rows, gown, gp, self_low, back_own, *pairs, near)
    gathered, own = lax.optimization_barrier((gathered, own))
    other = exchange(gathered, flips(groups[0])[1])
    grad_features = pl.pallas_call(
        functools.partial(last_scatter_kernel, [(n_inner - 2, 0, 0), (n_inner - 1, 1, 0)]),
        out_shape=shape(nrows, width),
        in_specs=[SM, SM] + [VM] * 5,
        out_specs=VM,
        scratch_shapes=[pltpu.VMEM((nrows, width), F32)],
        compiler_params=params(16),
        cost_estimate=cost(2 * 10**8, 2 * 10**6),
        name="scatter_last",
    )(hub_rows, send_count, send_rows, own, hub_grad, *direct)
    factor = 1.0 / float(nrows * ndevice) ** 0.5
    total_self, total_neigh, total_bias = pl.pallas_call(
        functools.partial(finish_kernel, steps, n_inner, factor),
        out_shape=(shape(width, width, dtype=F32),) * 2 + (shape(1, width, dtype=F32),),
        in_specs=[VM] * 3,
        out_specs=(VM,) * 3,
        scratch_shapes=[pltpu.VMEM((2 * width, width), F32)],
        compiler_params=params(16),
        cost_estimate=cost(10**6, 3 * 10**6),
        name="finish",
    )(gathered, other, bias_sum)
    return hidden_out, grad_features, total_self, total_neigh, total_bias.reshape(width)


def solution(mesh):
    both = ("outer", "inner")
    return jax.shard_map(
        body,
        mesh=mesh,
        in_specs=(
            P(both, None),
            P(both, None, None),
            P(both, None),
            P(both, None),
            P(both, None),
            P(both),
            P(),
            P(),
            P(),
            P(both, None),
        ),
        out_specs=(P(both, None), P(both, None), P(), P(), P()),
        check_vma=False,
    )
```
